32 devices in a mesh: groups: 2 (over y), dp: 16 (over z, x, core).
Axes of the slice: x: 2, y: 2, z: 4, core: 2. Of those that a mesh axis runs over, the one named last changes fastest.
Arguments:
- queries: bfloat16 [32, 128, 8192], P(('groups', 'dp')), parts along dimension 0, may hold values from -30 to 30
- fresh_kv: bfloat16 [32, 128, 2, 512], P(('groups', 'dp')), parts along dimension 0, may hold values from -13 to 13
- kv_pool: bfloat16 [4096, 2, 8, 512], P(('groups', 'dp')), parts along dimension 0, may hold values from -6 to 6
- page_holder: int32 [32, 128], P(('groups', 'dp')), parts along dimension 0, may hold values from 0 to 15, as said below
- page_slot: int32 [32, 128], P(('groups', 'dp')), parts along dimension 0, may hold values from 0 to 127, as said below
- cached_len: int32 [32], P(('groups', 'dp')), parts along dimension 0, may hold values from 768 to 1024, as said below
- fresh_len: int32 [32], P(('groups', 'dp')), parts along dimension 0, may hold values from 64 to 128, as said below
Outputs:
- attended: bfloat16 [32, 128, 8192], P(('groups', 'dp')), parts along dimension 0
The draws below stay inside these ranges and needn't reach their ends.
There are 2 independent parts, one for each index of `groups`. The reference program is written for one: setup_inputs(seed, part) draws one part's arguments, and reference() takes and returns one part's arrays. A program takes and returns all parts, laid end to end along the dimension named above; each array names one. Nothing has to cross between parts.
Inputs may be any that keep to these rules, and one draw needn't show every extreme that they name: `page_holder`: each pool device holds exactly 8 of the 128 pages of every trajectory; for one page index j no two trajectories have the same holder. `page_slot`: no two pages of the group share a (holder, slot) pair, so every slot of every pool is used. `cached_len`: some trajectory has the most. `fresh_len`: some trajectory has the most.
All inputs are finite; a program needn't handle non-finite values.
Results may differ from the reference program's by a relative error of at most 0.0031.
Values may be sent and summed in bfloat16 or wider, within the bound.
No kernel may reach another device: no remote copies, remote signals or barrier semaphores. Data moves between devices by JAX's collectives and lax.ppermute only.
A program may use at most 128 MiB of HBM per device.

```python
import jax
import jax.numpy as jnp
from jax import lax

H = 64
KVH = 4
HD = 128
PAGE = 8
MP = 128
C = 128
TRAJ = 16
POOL = 128


def page_places(key):
    cycle_key, seat_key, order_key, slot_key = jax.random.split(key, 4)
    cycle_order = jax.random.permutation(cycle_key, TRAJ)
    start_seat = jax.random.permutation(seat_key, TRAJ)
    page_order = jax.random.permutation(order_key, MP)
    holder = cycle_order[(start_seat[:, None] + page_order[None, :]) % TRAJ]
    slot_perms = jax.vmap(lambda one_key: jax.random.permutation(one_key, POOL))(jax.random.split(slot_key, TRAJ))
    slot_ids = slot_perms[holder, jnp.arange(MP)[None, :]]
    return (holder.astype(jnp.int32), slot_ids.astype(jnp.int32))


def draw_queries(key, part):
    key = jax.random.fold_in(key, 1)
    first = jax.random.fold_in(key, 0)
    shape = (TRAJ, C, KVH, H // KVH, HD)
    values = jnp.clip(2.5 * jax.random.normal(first, shape, jnp.float32), -15.0, 15.0)
    return values.reshape(TRAJ, C, H * HD).astype(jnp.bfloat16)


def draw_fresh_kv(key, part):
    key = jax.random.fold_in(key, 2)
    first = jax.random.fold_in(key, 0)
    shape = (TRAJ, C, 2, KVH, HD)
    values = jnp.clip(jax.random.normal(first, shape, jnp.float32), -6.0, 6.0)
    return values.reshape(TRAJ, C, 2, KVH * HD).astype(jnp.bfloat16)


def draw_kv_pool(key, part):
    key = jax.random.fold_in(key, 3)
    first = jax.random.fold_in(key, 0)
    shape = (TRAJ * POOL, 2, PAGE, KVH * HD)
    values = jnp.clip(jax.random.normal(first, shape, jnp.float32), -6.0, 6.0)
    return values.astype(jnp.bfloat16)


def draw_page_holder(key, part):
    holder, slot_ids = page_places(key)
    return holder


def draw_page_slot(key, part):
    holder, slot_ids = page_places(key)
    return slot_ids


def draw_cached_len(key, part):
    key = jax.random.fold_in(key, 5)
    draw_key, pick_key = jax.random.split(key, 2)
    lengths = jax.random.randint(draw_key, (TRAJ,), 3 * MP * PAGE // 4, MP * PAGE + 1)
    longest = jax.random.randint(pick_key, (), 0, TRAJ)
    return jnp.where(jnp.arange(TRAJ) == longest, MP * PAGE, lengths).astype(jnp.int32)


def draw_fresh_len(key, part):
    key = jax.random.fold_in(key, 6)
    draw_key, pick_key = jax.random.split(key, 2)
    lengths = jax.random.randint(draw_key, (TRAJ,), C // 2, C + 1)
    longest = jax.random.randint(pick_key, (), 0, TRAJ)
    return jnp.where(jnp.arange(TRAJ) == longest, C, lengths).astype(jnp.int32)


def setup_inputs(seed: int = 0, part: int = 0) -> dict:
    splits = jax.random.split(jax.random.key(seed), 8)
    part_splits = jax.random.split(jax.random.fold_in(splits[7], part), 8)
    return {
        "queries": draw_queries(jax.random.fold_in(jax.random.fold_in(splits[7], part), 71), part),
        "fresh_kv": draw_fresh_kv(jax.random.fold_in(jax.random.fold_in(splits[7], part), 71), part),
        "kv_pool": draw_kv_pool(jax.random.fold_in(jax.random.fold_in(splits[7], part), 71), part),
        "page_holder": draw_page_holder(jax.random.fold_in(jax.random.fold_in(splits[7], part), 71), part),
        "page_slot": draw_page_slot(jax.random.fold_in(jax.random.fold_in(splits[7], part), 71), part),
        "cached_len": draw_cached_len(jax.random.fold_in(jax.random.fold_in(splits[7], part), 71), part),
        "fresh_len": draw_fresh_len(jax.random.fold_in(jax.random.fold_in(splits[7], part), 71), part),
    }


def reference(queries, fresh_kv, kv_pool, page_holder, page_slot, cached_len, fresh_len):
    inv_root = HD ** -0.5
    group_size = H // KVH

    def per_trajectory(pieces):
        query, fresh, holder, slot_ids, length, filled = pieces
        pool_rows = (holder * POOL + slot_ids).astype(jnp.int32)
        cached = kv_pool[pool_rows]
        all_keys = jnp.concatenate([cached[:, 0].reshape(MP * PAGE, KVH, HD), fresh[:, 0].reshape(C, KVH, HD)], axis=0).astype(jnp.float32)
        all_values = jnp.concatenate([cached[:, 1].reshape(MP * PAGE, KVH, HD), fresh[:, 1].reshape(C, KVH, HD)], axis=0).astype(jnp.float32)
        query_wide = query.reshape(C, KVH, group_size, HD).astype(jnp.float32)
        scores = jnp.einsum('cghd,ngd->cghn', query_wide, all_keys) * inv_root
        position = jnp.arange(MP * PAGE + C, dtype=jnp.int32)
        row_ids = jnp.arange(C, dtype=jnp.int32)
        allowed = jnp.where(position[None, :] < MP * PAGE, (position < length)[None, :], (position[None, :] - MP * PAGE) <= row_ids[:, None])
        scores = jnp.where(allowed[:, None, None, :], scores, -jnp.inf)
        top_score = jnp.max(scores, axis=-1, keepdims=True)
        weights = jnp.exp(scores - top_score)
        weight_sum = jnp.sum(weights, axis=-1, keepdims=True)
        rounded = lax.optimization_barrier(weights.astype(jnp.bfloat16)).astype(jnp.float32)
        mixed_out = jnp.einsum('cghn,ngd->cghd', rounded, all_values) / weight_sum
        row_live = (row_ids < filled)[:, None, None, None]
        return jnp.where(row_live, mixed_out, 0.0).reshape(C, H * HD).astype(jnp.bfloat16)

    return lax.map(per_trajectory, (queries, fresh_kv, page_holder, page_slot, cached_len, fresh_len))
```

```python
import functools

import jax
import jax.numpy as jnp
from jax import lax
from jax.experimental import pallas as pl
from jax.experimental.pallas import tpu as pltpu
from jax.sharding import PartitionSpec as P

H = 64
KVH = 4
HD = 128
PAGE = 8
MP = 128
C = 128
GROUP = H // KVH
LOG2E = 1.4426950408889634
NEG = -1e30


def gather_kernel(outgoing_ref, pool_ref, *out_refs):
    devices, capacity = out_refs[0].shape[0], out_refs[0].shape[2]

    def step(t, carry):
        for r in range(capacity):
            page = pool_ref[outgoing_ref[t * capacity + r]]
            for h in range(KVH):
                out_refs[h][t, :, r] = page[:, :, h * HD : (h + 1) * HD]
        return carry

    lax.fori_loop(0, devices, step, 0)


def gather_pages(kv_pool, outgoing, devices):
    capacity = MP // devices
    piece = jax.ShapeDtypeStruct((devices, 2, capacity, PAGE, HD), kv_pool.dtype)
    return pl.pallas_call(
        gather_kernel,
        out_shape=(piece,) * KVH,
        in_specs=[
            pl.BlockSpec(memory_space=pltpu.SMEM),
            pl.BlockSpec(memory_space=pltpu.VMEM),
        ],
        out_specs=(pl.BlockSpec(memory_space=pltpu.VMEM),) * KVH,
        compiler_params=pltpu.CompilerParams(vmem_limit_bytes=24 * 2**20),
        cost_estimate=pl.CostEstimate(
            flops=0, bytes_accessed=2 * kv_pool.size * 2, transcendentals=0
        ),
        name="gather_pages",
    )(outgoing, kv_pool)


def attend_kernel(
    filled_ref, bias_ref, q_ref, k_ref, v_ref, fk_ref, fv_ref, *rest, heads
):
    o_ref = rest[-1]
    scale = HD**-0.5 * LOG2E
    rows = heads * C
    k = k_ref[...].reshape(MP * PAGE, HD)
    v = v_ref[...].reshape(MP * PAGE, HD)
    fk = fk_ref[...]
    fv = fv_ref[...]
    bias = bias_ref[...]
    nt = (((1,), (1,)), ((), ()))
    token = lax.rem(lax.broadcasted_iota(jnp.int32, (rows, C), 0), C)
    causal = lax.broadcasted_iota(jnp.int32, (rows, C), 1) <= token
    live = token[:, :HD] < filled_ref[0]
    for g in range(0, GROUP, heads):
        q = jnp.concatenate(
            [q_ref[:, (g + i) * HD : (g + i + 1) * HD] for i in range(heads)], axis=0
        )
        s1 = lax.dot_general(q, k, nt, preferred_element_type=jnp.float32) + bias
        s2 = lax.dot_general(q, fk, nt, preferred_element_type=jnp.float32)
        s2 = jnp.where(causal, s2, NEG)
        top = jnp.maximum(
            jnp.max(s1, axis=1, keepdims=True), jnp.max(s2, axis=1, keepdims=True)
        )
        p1 = jnp.exp2((s1 - top) * scale)
        p2 = jnp.exp2((s2 - top) * scale)
        total = jnp.sum(p1, axis=1, keepdims=True) + jnp.sum(p2, axis=1, keepdims=True)
        o = jnp.dot(p1.astype(jnp.bfloat16), v, preferred_element_type=jnp.float32)
        o += jnp.dot(p2.astype(jnp.bfloat16), fv, preferred_element_type=jnp.float32)
        o = jnp.where(live, o * (1.0 / total), 0.0).astype(o_ref.dtype)
        for i in range(heads):
            o_ref[:, (g + i) * HD : (g + i + 1) * HD] = o[i * C : (i + 1) * C]


def attend(h, filled, bias, queries, pages, fresh_k, fresh_v, out):
    width = GROUP * HD
    devices = pages.shape[0]
    tokens = MP * PAGE // devices
    pages = pages.reshape(devices, 2, tokens, HD)
    operands = [filled, bias, queries, pages, pages, fresh_k, fresh_v]
    in_specs = [
        pl.BlockSpec(memory_space=pltpu.SMEM),
        pl.BlockSpec((1, MP * PAGE), lambda i: (0, 0)),
        pl.BlockSpec((C, width), lambda i: (0, h)),
        pl.BlockSpec((devices, None, tokens, HD), lambda i: (0, 0, 0, 0)),
        pl.BlockSpec((devices, None, tokens, HD), lambda i: (0, 1, 0, 0)),
        pl.BlockSpec((C, HD), lambda i: (0, h)),
        pl.BlockSpec((C, HD), lambda i: (0, h)),
    ]
    aliases = {}
    if out is not None:
        operands.append(out)
        in_specs.append(pl.BlockSpec(memory_space=pl.ANY))
        aliases = {len(operands) - 1: 0}
    return pl.pallas_call(
        functools.partial(attend_kernel, heads=2),
        grid=(1,),
        out_shape=jax.ShapeDtypeStruct((C, H * HD), jnp.bfloat16),
        in_specs=in_specs,
        out_specs=pl.BlockSpec((C, width), lambda i: (0, h)),
        input_output_aliases=aliases,
        compiler_params=pltpu.CompilerParams(vmem_limit_bytes=32 * 2**20),
        cost_estimate=pl.CostEstimate(
            flops=4 * C * width * (MP * PAGE + C),
            bytes_accessed=4 * C * width * 2,
            transcendentals=C * GROUP * (MP * PAGE + C),
        ),
        name=f"attend_{h}",
    )(*operands)


def local(queries, fresh_kv, kv_pool, page_holder, page_slot, cached_len, fresh_len):
    devices = lax.axis_size("dp")
    capacity = MP // devices
    holder, slot = page_holder[0], page_slot[0]
    page = jnp.arange(MP, dtype=jnp.int32)
    same = holder[:, None] == holder[None, :]
    rank = jnp.sum((same & (page[None, :] < page[:, None])).astype(jnp.int32), axis=1)
    hits = (holder * capacity + rank)[:, None] == page[None, :]
    asked = jnp.sum(jnp.where(hits, slot[:, None], 0), axis=0).reshape(devices, capacity)
    outgoing = lax.all_to_all(asked, "dp", split_axis=0, concat_axis=0, tiled=True)
    pieces = gather_pages(kv_pool, outgoing.reshape(MP), devices)
    received = [
        lax.all_to_all(piece, "dp", split_axis=0, concat_axis=0, tiled=True)
        for piece in pieces
    ]
    arrived = jnp.sum(jnp.where(hits, page[:, None], 0), axis=0)
    place = arrived[:, None] * PAGE + jnp.arange(PAGE, dtype=jnp.int32)[None, :]
    bias = jnp.where(place < cached_len[0], 0.0, NEG).astype(jnp.float32)
    bias = bias.reshape(1, MP * PAGE)
    fresh_k, fresh_v = fresh_kv[0, :, 0], fresh_kv[0, :, 1]
    out = None
    for h in range(KVH):
        out = attend(
            h, fresh_len, bias, queries[0], received[h], fresh_k, fresh_v, out
        )
    return out[None]


def solution(mesh):
    return jax.shard_map(
        local,
        mesh=mesh,
        in_specs=(
            P(("groups", "dp"), None, None),
            P(("groups", "dp"), None, None, None),
            P(("groups", "dp"), None, None, None),
            P(("groups", "dp"), None),
            P(("groups", "dp"), None),
            P(("groups", "dp")),
            P(("groups", "dp")),
        ),
        out_specs=P(("groups", "dp"), None, None),
        check_vma=False,
    )
```

```python
import functools

import jax
import jax.numpy as jnp
from jax import lax
from jax.experimental import pallas as pl
from jax.experimental.pallas import tpu as pltpu
from jax.sharding import PartitionSpec as P

H = 64
KVH = 4
HD = 128
PAGE = 8
MP = 128
C = 128
GROUP = H // KVH
LOG2E = 1.4426950408889634
NEG = -1e30
CHUNKS = ((0, 3), (3, 1))
MOST_PERMUTES = 8


def ask_kernel(me_ref, holder_ref, slot_ref, asked_ref):
    chips = asked_ref.shape[0]
    capacity = MP // (2 * chips)
    core = me_ref[0] & 1
    square = (MP, MP)
    row = lax.broadcasted_iota(jnp.int32, square, 0)
    lane = lax.broadcasted_iota(jnp.int32, square, 1)
    holder = jnp.broadcast_to(holder_ref[...], square)
    same = (holder.T == holder) & (row < lane)
    rank = jnp.sum(same.astype(jnp.int32), axis=0, keepdims=True)
    low = (holder_ref[...] & 1 ^ core) * capacity + rank
    packed = jnp.broadcast_to(low * MP + slot_ref[...], square).T
    slots = jnp.where(packed // MP == lane, packed % MP, 0)
    chip = lax.broadcasted_iota(jnp.int32, (chips, MP), 0)
    of_chip = jnp.broadcast_to(holder_ref[...] >> 1, (chips, MP)) == chip
    asked = jnp.dot(
        of_chip.astype(jnp.float32).astype(jnp.bfloat16),
        slots.astype(jnp.float32).astype(jnp.bfloat16),
        preferred_element_type=jnp.float32,
    )
    asked_ref[...] = asked.astype(jnp.int32).reshape(chips, 1, MP)


def ask(me, page_holder, page_slot, chips):
    return pl.pallas_call(
        ask_kernel,
        out_shape=jax.ShapeDtypeStruct((chips, 1, MP), jnp.int32),
        in_specs=[
            pl.BlockSpec(memory_space=pltpu.SMEM),
            pl.BlockSpec(memory_space=pltpu.VMEM),
            pl.BlockSpec(memory_space=pltpu.VMEM),
        ],
        out_specs=pl.BlockSpec(memory_space=pltpu.VMEM),
        name="ask",
    )(me, page_holder, page_slot)


def live_kernel(order_ref, length_ref, holder_ref, live_ref, *, capacity):
    square = (MP, MP)
    row = lax.broadcasted_iota(jnp.int32, square, 0)
    lane = lax.broadcasted_iota(jnp.int32, square, 1)
    holder = jnp.broadcast_to(holder_ref[...], square)
    same = (holder.T == holder) & (row < lane)
    rank = jnp.sum(same.astype(jnp.int32), axis=0, keepdims=True)
    place = (holder_ref[...] ^ order_ref[0]) * capacity + rank
    hits = jnp.broadcast_to(place, square) == row
    page = jnp.sum(jnp.where(hits, lane, 0), axis=1, keepdims=True)
    page = jnp.broadcast_to(page, square)
    shape = (MP, PAGE, HD)
    token = page[:, None, :] * PAGE + lax.broadcasted_iota(jnp.int32, shape, 1)
    live = jnp.where(token < length_ref[0], 1.0, 0.0)
    live_ref[...] = live.reshape(MP * PAGE, HD).astype(live_ref.dtype)


def live_tokens(order, cached_len, page_holder, capacity):
    return pl.pallas_call(
        functools.partial(live_kernel, capacity=capacity),
        out_shape=jax.ShapeDtypeStruct((MP * PAGE, HD), jnp.bfloat16),
        in_specs=[
            pl.BlockSpec(memory_space=pltpu.SMEM),
            pl.BlockSpec(memory_space=pltpu.SMEM),
            pl.BlockSpec(memory_space=pltpu.VMEM),
        ],
        out_specs=pl.BlockSpec(memory_space=pltpu.VMEM),
        name="live_tokens",
    )(order, cached_len, page_holder)


def gather_kernel(mine_ref, wanted_ref, own_ref, mate_ref, *out_refs, flip):
    whole = len(out_refs) == len(CHUNKS)
    chips, capacity = wanted_ref.shape[0], out_refs[0].shape[-3] // 2

    def copy(x, asker):
        for b, pool_ref in enumerate((own_ref, mate_ref)):
            for r in range(capacity):
                n = b * capacity + r
                page = pool_ref[wanted_ref[asker, 0, n]]
                for c, (first, count) in enumerate(CHUNKS):
                    out_ref = out_refs[c] if whole else out_refs[c * chips + x]
                    for h in range(count):
                        cols = slice((first + h) * HD, (first + h + 1) * HD)
                        if whole:
                            out_ref[x, h, :, n] = page[:, :, cols]
                        else:
                            out_ref[h, :, n] = page[:, :, cols]

    if whole:
        pl.loop(0, chips)(lambda x: copy(x, x))
    else:
        for x in range(chips):
            copy(x, mine_ref[0] ^ x)


def gather_pages(mine, wanted, own, mate, flip):
    chips = wanted.shape[0]
    places = MP // chips
    shapes = []
    for first, count in CHUNKS:
        shape = (count, 2, places, PAGE, HD)
        shapes += [shape] * chips if flip else [(chips,) + shape]
    pool = pl.BlockSpec(memory_space=pltpu.VMEM)
    return pl.pallas_call(
        functools.partial(gather_kernel, flip=flip),
        out_shape=[jax.ShapeDtypeStruct(shape, own.dtype) for shape in shapes],
        in_specs=[
            pl.BlockSpec(memory_space=pltpu.SMEM),
            pl.BlockSpec(memory_space=pltpu.SMEM),
            pool,
            pool,
        ],
        out_specs=[pl.BlockSpec(memory_space=pltpu.VMEM)] * len(shapes),
        compiler_params=pltpu.CompilerParams(vmem_limit_bytes=32 * 2**20),
        cost_estimate=pl.CostEstimate(
            flops=0, bytes_accessed=4 * own.size * 2, transcendentals=0
        ),
        name="gather_pages",
    )(mine, wanted, own, mate)


def attend_kernel(filled_ref, live_ref, q_ref, fk_ref, fv_ref, *rest, parts, heads):
    piece_refs = rest[:parts]
    o_ref, k_ref, v_ref = rest[-3:]
    scale = HD**-0.5 * LOG2E
    rows = heads * C
    tokens = piece_refs[0].shape[-2]
    cached = parts * tokens
    fk = fk_ref[...]
    for p in range(parts):
        at = slice(p * tokens, (p + 1) * tokens)
        live = live_ref[at]
        k_ref[at] = jnp.where(live > 0, piece_refs[p][0], fk[:1])
        v_ref[at, :HD] = jnp.where(live > 0, piece_refs[p][1], jnp.zeros_like(live))
        v_ref[at, HD:] = live
    k_ref[cached:] = fk
    v_ref[cached:, :HD] = fv_ref[...]
    v_ref[cached:, HD:] = jnp.ones_like(fk)
    nt = (((1,), (1,)), ((), ()))
    token = lax.rem(lax.broadcasted_iota(jnp.int32, (rows, C), 0), C)
    causal = lax.broadcasted_iota(jnp.int32, (rows, C), 1) <= token
    filled = token < filled_ref[0]
    for g in range(0, q_ref.shape[1] // HD, heads):
        q = jnp.concatenate(
            [q_ref[:, (g + i) * HD : (g + i + 1) * HD] for i in range(heads)], axis=0
        )
        s = lax.dot_general(q, k_ref[...], nt, preferred_element_type=jnp.float32)
        s1, s2 = s[:, :cached], jnp.where(causal, s[:, cached:], NEG)
        top = jnp.maximum(
            jnp.max(s1, axis=1, keepdims=True), jnp.max(s2, axis=1, keepdims=True)
        )
        p1 = jnp.exp2((s1 - top) * scale).astype(jnp.bfloat16)
        p2 = jnp.exp2((s2 - top) * scale).astype(jnp.bfloat16)
        o = jnp.dot(
            jnp.concatenate([p1, p2], axis=1),
            v_ref[...],
            preferred_element_type=jnp.float32,
        )
        o = jnp.where(filled, o[:, :HD] / o[:, HD:], 0.0).astype(o_ref.dtype)
        for i in range(heads):
            o_ref[:, (g + i) * HD : (g + i + 1) * HD] = o[i * C : (i + 1) * C]


def attend(first, filled, live, queries, fresh_k, fresh_v, pieces, out):
    width = GROUP * HD
    operands = [filled, live, queries, fresh_k, fresh_v]
    in_specs = [
        pl.BlockSpec(memory_space=pltpu.SMEM),
        pl.BlockSpec((MP * PAGE, HD), lambda h: (0, 0)),
        pl.BlockSpec((C, width), lambda h: (0, h + first)),
        pl.BlockSpec((C, HD), lambda h: (0, h + first)),
        pl.BlockSpec((C, HD), lambda h: (0, h + first)),
    ]
    parts = 0
    for piece in pieces:
        sources = piece.shape[0] if piece.ndim == 5 else 1
        for i in range(sources):
            operands.append(piece)
            if piece.ndim == 5:
                in_specs.append(
                    pl.BlockSpec(
                        (None, None) + piece.shape[2:],
                        lambda h, i=i: (i, h, 0, 0, 0),
                    )
                )
            else:
                in_specs.append(
                    pl.BlockSpec((None,) + piece.shape[1:], lambda h: (h, 0, 0, 0))
                )
        parts += sources
    count = pieces[0].shape[-4]
    aliases = {}
    if out is not None:
        operands.append(out)
        in_specs.append(pl.BlockSpec(memory_space=pl.ANY))
        aliases = {len(operands) - 1: 0}
    keys = MP * PAGE + C
    return pl.pallas_call(
        functools.partial(attend_kernel, parts=parts, heads=4),
        grid=(count,),
        out_shape=jax.ShapeDtypeStruct((C, H * HD), jnp.bfloat16),
        in_specs=in_specs,
        out_specs=pl.BlockSpec((C, width), lambda h: (0, h + first)),
        scratch_shapes=[
            pltpu.VMEM((keys, HD), jnp.bfloat16),
            pltpu.VMEM((keys, 2 * HD), jnp.bfloat16),
        ],
        input_output_aliases=aliases,
        compiler_params=pltpu.CompilerParams(vmem_limit_bytes=40 * 2**20),
        cost_estimate=pl.CostEstimate(
            flops=4 * count * C * width * keys,
            bytes_accessed=4 * count * C * width * 2,
            transcendentals=count * C * GROUP * keys,
        ),
        name=f"attend_{first}",
    )(*operands)


def local(queries, fresh_kv, kv_pool, page_holder, page_slot, cached_len, fresh_len):
    devices = lax.axis_size("dp")
    chips = devices // 2
    me = lax.axis_index("dp")
    flip = chips <= MOST_PERMUTES
    same_core = [[2 * i + core for i in range(chips)] for core in range(2)]
    mate_pool = lax.ppermute(kv_pool, "dp", [(i, i ^ 1) for i in range(devices)])
    asked = ask(me.reshape(1), page_holder, page_slot, chips)
    exchange = functools.partial(
        lax.all_to_all,
        axis_name="dp",
        split_axis=0,
        concat_axis=0,
        axis_index_groups=same_core,
        tiled=True,
    )
    wanted = exchange(asked)
    mine = (me // 2).reshape(1)
    gathered = gather_pages(mine, wanted, kv_pool, mate_pool, flip)
    order = (me if flip else me & 1).reshape(1)
    live = live_tokens(order, cached_len, page_holder, MP // devices)
    fresh_k, fresh_v = fresh_kv[0, :, 0], fresh_kv[0, :, 1]
    out = None
    for c, (first, count) in enumerate(CHUNKS):
        if flip:
            pieces = list(gathered[c * chips : (c + 1) * chips])
            for x in reversed(range(1, chips)):
                pairs = [(i, i ^ (2 * x)) for i in range(devices)]
                pieces[x] = lax.ppermute(pieces[x], "dp", pairs)
        else:
            pieces = [exchange(gathered[c])]
        tokens = pieces[0].shape[-3] * PAGE
        pieces = [p.reshape(p.shape[:-3] + (tokens, HD)) for p in pieces]
        out = attend(first, fresh_len, live, queries[0], fresh_k, fresh_v, pieces, out)
    return out[None]


def solution(mesh):
    return jax.shard_map(
        local,
        mesh=mesh,
        in_specs=(
            P(("groups", "dp"), None, None),
            P(("groups", "dp"), None, None, None),
            P(("groups", "dp"), None, None, None),
            P(("groups", "dp"), None),
            P(("groups", "dp"), None),
            P(("groups", "dp")),
            P(("groups", "dp")),
        ),
        out_specs=P(("groups", "dp"), None, None),
        check_vma=False,
    )
```

```python
import functools

import jax
import jax.numpy as jnp
from jax import lax
from jax.experimental import pallas as pl
from jax.experimental.pallas import tpu as pltpu
from jax.sharding import PartitionSpec as P

H = 64
KVH = 4
HD = 128
PAGE = 8
MP = 128
C = 128
GROUP = H // KVH
LOG2E = 1.4426950408889634
NEG = -1e30
CHUNKS = ((0, 2), (2, 2))
MOST_PERMUTES = 8


def ask_kernel(me_ref, holder_ref, slot_ref, asked_ref):
    chips = asked_ref.shape[0]
    capacity = MP // (2 * chips)
    core = me_ref[0] & 1
    square = (MP, MP)
    row = lax.broadcasted_iota(jnp.int32, square, 0)
    lane = lax.broadcasted_iota(jnp.int32, square, 1)
    holder = jnp.broadcast_to(holder_ref[...], square)
    same = (holder.T == holder) & (row < lane)
    rank = jnp.sum(same.astype(jnp.int32), axis=0, keepdims=True)
    low = (holder_ref[...] & 1 ^ core) * capacity + rank
    packed = jnp.broadcast_to(low * MP + slot_ref[...], square).T
    slots = jnp.where(packed // MP == lane, packed % MP, 0)
    chip = lax.broadcasted_iota(jnp.int32, (chips, MP), 0)
    of_chip = jnp.broadcast_to(holder_ref[...] >> 1, (chips, MP)) == chip
    asked = jnp.dot(
        of_chip.astype(jnp.float32).astype(jnp.bfloat16),
        slots.astype(jnp.float32).astype(jnp.bfloat16),
        preferred_element_type=jnp.float32,
    )
    asked_ref[...] = asked.astype(jnp.int32).reshape(chips, 1, MP)


def ask(me, page_holder, page_slot, chips):
    return pl.pallas_call(
        ask_kernel,
        out_shape=jax.ShapeDtypeStruct((chips, 1, MP), jnp.int32),
        in_specs=[
            pl.BlockSpec(memory_space=pltpu.SMEM),
            pl.BlockSpec(memory_space=pltpu.VMEM),
            pl.BlockSpec(memory_space=pltpu.VMEM),
        ],
        out_specs=pl.BlockSpec(memory_space=pltpu.VMEM),
        name="ask",
    )(me, page_holder, page_slot)


def live_kernel(order_ref, length_ref, holder_ref, live_ref, *, capacity):
    square = (MP, MP)
    row = lax.broadcasted_iota(jnp.int32, square, 0)
    lane = lax.broadcasted_iota(jnp.int32, square, 1)
    holder = jnp.broadcast_to(holder_ref[...], square)
    same = (holder.T == holder) & (row < lane)
    rank = jnp.sum(same.astype(jnp.int32), axis=0, keepdims=True)
    place = (holder_ref[...] ^ order_ref[0]) * capacity + rank
    hits = jnp.broadcast_to(place, square) == row
    page = jnp.sum(jnp.where(hits, lane, 0), axis=1, keepdims=True)
    page = jnp.broadcast_to(page, square)
    shape = (MP, PAGE, HD)
    token = page[:, None, :] * PAGE + lax.broadcasted_iota(jnp.int32, shape, 1)
    live = jnp.where(token < length_ref[0], 1.0, 0.0)
    live_ref[...] = live.reshape(MP * PAGE, HD).astype(live_ref.dtype)


def live_tokens(order, cached_len, page_holder, capacity):
    return pl.pallas_call(
        functools.partial(live_kernel, capacity=capacity),
        out_shape=pltpu.VMEM((MP * PAGE, HD), jnp.bfloat16),
        in_specs=[
            pl.BlockSpec(memory_space=pltpu.SMEM),
            pl.BlockSpec(memory_space=pltpu.SMEM),
            pl.BlockSpec(memory_space=pltpu.VMEM),
        ],
        out_specs=pl.BlockSpec(memory_space=pltpu.VMEM),
        name="live_tokens",
    )(order, cached_len, page_holder)


def gather_kernel(mine_ref, wanted_ref, own_ref, mate_ref, *rest, pieces):
    out_refs = rest[: len(pieces)]
    held_refs = rest[len(pieces) : -2]
    load_sem, store_sem = rest[-2:]
    chips = wanted_ref.shape[0]
    capacity = out_refs[0].shape[-3] // 2
    whole = pieces[0][0] is None
    places = range(chips)[::-1]

    def parts_of(x):
        return [i for i, piece in enumerate(pieces) if whole or piece[0] == x]

    def place_of(i, x, asker, n):
        held_ref = held_refs[i].at[asker] if whole else held_refs[i]
        return held_ref.at[:, n]

    def columns(i):
        _, first, count = pieces[i]
        return pl.ds(first * HD, count * HD)

    def loads(x, asker):
        for n in range(capacity):
            for i in parts_of(x):
                yield pltpu.make_async_copy(
                    own_ref.at[wanted_ref[asker, 0, n], :, :, columns(i)],
                    place_of(i, x, asker, n),
                    load_sem.at[0 if whole else x],
                )

    def copy(x, asker):
        for n in range(capacity, 2 * capacity):
            page_ref = mate_ref.at[wanted_ref[asker, 0, n]]
            for i in parts_of(x):
                place_of(i, x, asker, n)[...] = page_ref[:, :, columns(i)]

    def store(i):
        return pltpu.make_async_copy(held_refs[i], out_refs[i], store_sem.at[i])

    if whole:

        @pl.loop(0, chips)
        def _(x):
            for load in loads(None, x):
                load.start()
            copy(None, x)
            for load in loads(None, x):
                load.wait()

        for i in range(len(pieces)):
            store(i).start()
    else:
        for x in places:
            for load in loads(x, mine_ref[0] ^ x):
                load.start()
        for x in places:
            copy(x, mine_ref[0] ^ x)
            for i in parts_of(x):
                half = held_refs[i].at[:, pl.ds(0, capacity)]
                pltpu.make_async_copy(half, half, load_sem.at[x]).wait()
            for i in parts_of(x):
                store(i).start()
    for i in range(len(pieces)):
        store(i).wait()


def gather_pages(mine, wanted, own, mate, pieces):
    chips = wanted.shape[0]
    shapes = []
    for x, _, count in pieces:
        shape = (2, MP // chips, PAGE, count * HD)
        shapes.append((chips,) + shape if x is None else shape)
    return pl.pallas_call(
        functools.partial(gather_kernel, pieces=tuple(pieces)),
        out_shape=[pltpu.HBM(shape, own.dtype) for shape in shapes],
        in_specs=[
            pl.BlockSpec(memory_space=pltpu.SMEM),
            pl.BlockSpec(memory_space=pltpu.SMEM),
            pl.BlockSpec(memory_space=pltpu.HBM),
            pl.BlockSpec(memory_space=pltpu.VMEM),
        ],
        out_specs=[pl.BlockSpec(memory_space=pltpu.HBM)] * len(pieces),
        scratch_shapes=[pltpu.VMEM(shape, own.dtype) for shape in shapes]
        + [
            pltpu.SemaphoreType.DMA((chips,)),
            pltpu.SemaphoreType.DMA((len(shapes),)),
        ],
        compiler_params=pltpu.CompilerParams(vmem_limit_bytes=24 * 2**20),
        cost_estimate=pl.CostEstimate(
            flops=0, bytes_accessed=2 * own.size * 2, transcendentals=0
        ),
        name="gather_pages",
    )(mine, wanted, own, mate)


def hold_back(pieces, after):
    anywhere = pl.BlockSpec(memory_space=pl.ANY)
    return pl.pallas_call(
        lambda *refs: None,
        out_shape=[pltpu.HBM(p.shape, p.dtype) for p in pieces],
        in_specs=[pl.BlockSpec(memory_space=pltpu.HBM)] * len(pieces)
        + [anywhere] * len(after),
        out_specs=[pl.BlockSpec(memory_space=pltpu.HBM)] * len(pieces),
        input_output_aliases={i: i for i in range(len(pieces))},
        name="hold_back",
    )(*pieces, *after)


def attend_kernel(filled_ref, live_ref, q_ref, fk_ref, fv_ref, *rest, parts, heads, fresh, earlier):
    piece_refs = rest[:parts]
    k_ref, v_ref = rest[-2:]
    rest = rest[parts:-2]
    if earlier:
        old_ref, stats_ref = rest[:2]
        o_ref = rest[-1]
    elif len(rest) == 2 and rest[0].dtype == jnp.float32:
        o_ref, stats_ref = rest
    else:
        o_ref = rest[-1]
    last = o_ref.dtype != jnp.float32
    scale = HD**-0.5 * LOG2E
    rows = heads * C
    tokens = piece_refs[0].shape[-2]
    cached = parts * tokens
    fk = fk_ref[...]
    for p in range(parts):
        at = slice(p * tokens, (p + 1) * tokens)
        live = live_ref[at]
        k_ref[at] = jnp.where(live > 0, piece_refs[p][0], fk[:1])
        v_ref[at, :HD] = jnp.where(live > 0, piece_refs[p][1], jnp.zeros_like(live))
        v_ref[at, HD:] = live
    if fresh:
        k_ref[cached:] = fk
        v_ref[cached:, :HD] = fv_ref[...]
        v_ref[cached:, HD:] = jnp.ones_like(fk)
    nt = (((1,), (1,)), ((), ()))
    token = lax.rem(lax.broadcasted_iota(jnp.int32, (rows, C), 0), C)
    lane = lax.broadcasted_iota(jnp.int32, (C, HD), 1)
    causal = lax.broadcasted_iota(jnp.int32, (rows, C), 1) <= token
    filled = token < filled_ref[0]
    if earlier:
        old_stats = stats_ref[...]
    elif not last:
        stats = jnp.zeros((C, HD), jnp.float32)
    for g in range(0, GROUP, heads):
        many = range(g, g + heads)
        cols = [slice(i * HD, (i + 1) * HD) for i in many]
        q = jnp.concatenate([q_ref[:, c] for c in cols], axis=0)
        s = lax.dot_general(q, k_ref[...], nt, preferred_element_type=jnp.float32)
        s1 = s[:, :cached]
        top = jnp.max(s1, axis=1, keepdims=True)
        if fresh:
            s2 = jnp.where(causal, s[:, cached:], NEG)
            top = jnp.maximum(top, jnp.max(s2, axis=1, keepdims=True))
        if earlier:
            old_top = jnp.concatenate([old_stats[:, i : i + 1] for i in many], axis=0)
            old_sum = jnp.concatenate(
                [old_stats[:, GROUP + i : GROUP + i + 1] for i in many], axis=0
            )
            top = jnp.maximum(top, old_top)
        p = jnp.exp2((s1 - top) * scale).astype(jnp.bfloat16)
        if fresh:
            p2 = jnp.exp2((s2 - top) * scale).astype(jnp.bfloat16)
            p = jnp.concatenate([p, p2], axis=1)
        o = jnp.dot(p, v_ref[...], preferred_element_type=jnp.float32)
        o, total = o[:, :HD], o[:, HD:]
        if earlier:
            share = jnp.exp2((old_top - top) * scale)
            old = jnp.concatenate([old_ref[:, c] for c in cols], axis=0)
            o = o + share * old
            total = total + share * old_sum
        if last:
            o = jnp.where(filled, o / total, 0.0).astype(o_ref.dtype)
        for k, i in enumerate(many):
            at = slice(k * C, (k + 1) * C)
            o_ref[:, cols[k]] = o[at]
            if not last:
                stats = jnp.where(lane == i, top[at], stats)
                stats = jnp.where(lane == GROUP + i, total[at], stats)
    if not last:
        stats_ref[...] = stats


def attend(first, count, filled, live, queries, fresh_k, fresh_v, pieces, rows, out=None, earlier=None, fresh=True, last=True):
    width = GROUP * HD
    tokens = sum(
        p.shape[-2] * (p.shape[0] if p.ndim == 4 else 1) for p, start in pieces
    )
    wide = pl.BlockSpec((C, width), lambda h: (0, h + first))
    narrow = pl.BlockSpec((C, HD), lambda h: (0, h + first))
    operands = [filled, live, queries, fresh_k, fresh_v]
    in_specs = [
        pl.BlockSpec(memory_space=pltpu.SMEM),
        pl.BlockSpec((tokens, HD), lambda h: (rows, 0)),
        wide,
        narrow,
        narrow,
    ]
    parts = 0
    for piece, start in pieces:
        low = first - start
        for i in range(piece.shape[0] if piece.ndim == 4 else 1):
            operands.append(piece)
            lead = (i,) if piece.ndim == 4 else ()
            block = (None,) * len(lead) + piece.shape[-3:-1] + (HD,)
            in_specs.append(
                pl.BlockSpec(block, lambda h, l=lead, d=low: l + (0, 0, h + d))
            )
            parts += 1
    if earlier is not None:
        operands += earlier
        in_specs += [wide, narrow]
    aliases = {}
    if out is not None:
        operands.append(out)
        in_specs.append(pl.BlockSpec(memory_space=pl.ANY))
        aliases = {len(operands) - 1: 0}
    if last:
        out_shape = jax.ShapeDtypeStruct((C, H * HD), jnp.bfloat16)
        out_specs = wide
    else:
        out_shape = [
            jax.ShapeDtypeStruct((C, H * HD), jnp.float32),
            jax.ShapeDtypeStruct((C, KVH * HD), jnp.float32),
        ]
        out_specs = [wide, narrow]
    keys = tokens + (C if fresh else 0)
    return pl.pallas_call(
        functools.partial(
            attend_kernel,
            parts=parts,
            heads=4,
            fresh=fresh,
            earlier=earlier is not None,
        ),
        grid=(count,),
        out_shape=out_shape,
        in_specs=in_specs,
        out_specs=out_specs,
        scratch_shapes=[
            pltpu.VMEM((keys, HD), jnp.bfloat16),
            pltpu.VMEM((keys, 2 * HD), jnp.bfloat16),
        ],
        input_output_aliases=aliases,
        compiler_params=pltpu.CompilerParams(vmem_limit_bytes=32 * 2**20),
        cost_estimate=pl.CostEstimate(
            flops=4 * count * C * width * keys,
            bytes_accessed=4 * count * C * width * 2,
            transcendentals=count * C * GROUP * keys,
        ),
        name=f"attend_{first}_{rows}",
    )(*operands)


def local(queries, fresh_kv, kv_pool, page_holder, page_slot, cached_len, fresh_len):
    devices = lax.axis_size("dp")
    chips = devices // 2
    me = lax.axis_index("dp")
    flip = chips <= MOST_PERMUTES
    same_core = [[2 * i + core for i in range(chips)] for core in range(2)]
    mate_pool = lax.ppermute(kv_pool, "dp", [(i, i ^ 1) for i in range(devices)])
    asked = ask(me.reshape(1), page_holder, page_slot, chips)
    exchange = functools.partial(
        lax.all_to_all,
        axis_name="dp",
        split_axis=0,
        concat_axis=0,
        axis_index_groups=same_core,
        tiled=True,
    )
    wanted = exchange(asked)
    own_pool = pltpu.with_memory_space_constraint(kv_pool, pltpu.HBM)
    mate_pool = pltpu.with_memory_space_constraint(mate_pool, pltpu.VMEM)
    mine = (me >> 1).reshape(1)
    gather = functools.partial(gather_pages, mine, wanted, own_pool, mate_pool)
    order = (me if flip else me & 1).reshape(1)
    live = live_tokens(order, cached_len, page_holder, MP // devices)
    fresh_k, fresh_v = fresh_kv[0, :, 0], fresh_kv[0, :, 1]

    def attend_some(first, count, pieces, *args, **kwargs):
        pieces = [
            (p.reshape(p.shape[:-3] + (-1, p.shape[-1])), start) for p, start in pieces
        ]
        return attend(
            first, count, fresh_len, live, queries[0], fresh_k, fresh_v, pieces, *args, **kwargs
        )

    out = None
    if not flip:
        sent = gather([(None, first, count) for first, count in CHUNKS])
        for (first, count), piece in zip(CHUNKS, sent):
            out = attend_some(first, count, [(exchange(piece), first)], 0, out)
        return out[None]

    def swap(piece, x):
        return lax.ppermute(piece, "dp", [(i, i ^ 2 * x) for i in range(devices)])

    near, far = range(chips // 2), range(chips // 2, chips)
    sent = gather(
        [(x, 0, KVH) for x in near]
        + [(x, first, count) for first, count in CHUNKS for x in far]
    )
    close = [(sent[x] if x == 0 else swap(sent[x], x), 0) for x in near]
    earlier = attend_some(0, KVH, close, 0, last=False)
    arrived = []
    for c, (first, count) in enumerate(CHUNKS):
        batch = sent[len(near) + c * len(far) : len(near) + (c + 1) * len(far)]
        if c > 0:
            batch = hold_back(batch, arrived[:2])
        arrived = [swap(piece, x) for piece, x in zip(batch, far)]
        pieces = [(piece, first) for piece in arrived]
        out = attend_some(
            first, count, pieces, 1, out, earlier=earlier, fresh=False
        )
    return out[None]


def solution(mesh):
    return jax.shard_map(
        local,
        mesh=mesh,
        in_specs=(
            P(("groups", "dp"), None, None),
            P(("groups", "dp"), None, None, None),
            P(("groups", "dp"), None, None, None),
            P(("groups", "dp"), None),
            P(("groups", "dp"), None),
            P(("groups", "dp")),
            P(("groups", "dp")),
        ),
        out_specs=P(("groups", "dp"), None, None),
        check_vma=False,
    )
```

```python
import functools

import jax
import jax.numpy as jnp
from jax import lax
from jax.experimental import pallas as pl
from jax.experimental.pallas import tpu as pltpu
from jax.sharding import PartitionSpec as P

H = 64
KVH = 4
HD = 128
PAGE = 8
MP = 128
C = 128
GROUP = H // KVH
LOG2E = 1.4426950408889634
NEG = -1e30
HEADS = 4
CHUNKS = ((0, 2), (2, 2))
MOST_PERMUTES = 8


def ask_kernel(me_ref, holder_ref, slot_ref, asked_ref):
    chips = asked_ref.shape[0]
    capacity = MP // (2 * chips)
    core = me_ref[0] & 1
    square = (MP, MP)
    row = lax.broadcasted_iota(jnp.int32, square, 0)
    lane = lax.broadcasted_iota(jnp.int32, square, 1)
    holder = jnp.broadcast_to(holder_ref[...], square)
    same = (holder.T == holder) & (row < lane)
    rank = jnp.sum(same.astype(jnp.int32), axis=0, keepdims=True)
    low = (holder_ref[...] & 1 ^ core) * capacity + rank
    packed = jnp.broadcast_to(low * MP + slot_ref[...], square).T
    slots = jnp.where(packed // MP == lane, packed % MP, 0)
    chip = lax.broadcasted_iota(jnp.int32, (chips, MP), 0)
    of_chip = jnp.broadcast_to(holder_ref[...] >> 1, (chips, MP)) == chip
    asked = jnp.dot(
        of_chip.astype(jnp.float32).astype(jnp.bfloat16),
        slots.astype(jnp.float32).astype(jnp.bfloat16),
        preferred_element_type=jnp.float32,
    )
    asked_ref[...] = asked.astype(jnp.int32).reshape(chips, 1, MP)


def ask(me, page_holder, page_slot, chips):
    return pl.pallas_call(
        ask_kernel,
        out_shape=jax.ShapeDtypeStruct((chips, 1, MP), jnp.int32),
        in_specs=[
            pl.BlockSpec(memory_space=pltpu.SMEM),
            pl.BlockSpec(memory_space=pltpu.VMEM),
            pl.BlockSpec(memory_space=pltpu.VMEM),
        ],
        out_specs=pl.BlockSpec(memory_space=pltpu.VMEM),
        name="ask",
    )(me, page_holder, page_slot)


def live_kernel(order_ref, length_ref, holder_ref, live_ref, *, capacity):
    square = (MP, MP)
    row = lax.broadcasted_iota(jnp.int32, square, 0)
    lane = lax.broadcasted_iota(jnp.int32, square, 1)
    holder = jnp.broadcast_to(holder_ref[...], square)
    same = (holder.T == holder) & (row < lane)
    rank = jnp.sum(same.astype(jnp.int32), axis=0, keepdims=True)
    place = (holder_ref[...] ^ order_ref[0]) * capacity + rank
    hits = jnp.broadcast_to(place, square) == row
    page = jnp.sum(jnp.where(hits, lane, 0), axis=1, keepdims=True)
    page = jnp.broadcast_to(page, square)
    shape = (MP, PAGE, HD)
    token = page[:, None, :] * PAGE + lax.broadcasted_iota(jnp.int32, shape, 1)
    live = jnp.where(token < length_ref[0], 1.0, 0.0)
    live_ref[...] = live.reshape(MP * PAGE, HD).astype(live_ref.dtype)


def live_tokens(order, cached_len, page_holder, capacity):
    return pl.pallas_call(
        functools.partial(live_kernel, capacity=capacity),
        out_shape=pltpu.VMEM((MP * PAGE, HD), jnp.bfloat16),
        in_specs=[
            pl.BlockSpec(memory_space=pltpu.SMEM),
            pl.BlockSpec(memory_space=pltpu.SMEM),
            pl.BlockSpec(memory_space=pltpu.VMEM),
        ],
        out_specs=pl.BlockSpec(memory_space=pltpu.VMEM),
        name="live_tokens",
    )(order, cached_len, page_holder)


def gather_kernel(mine_ref, wanted_ref, own_ref, mate_ref, *rest, pieces):
    out_refs = rest[: len(pieces)]
    held_refs = rest[len(pieces) : -2]
    load_sem, store_sem = rest[-2:]
    chips = wanted_ref.shape[0]
    capacity = out_refs[0].shape[-3] // 2
    whole = pieces[0][0] is None
    places = range(chips)[::-1]

    def parts_of(x):
        return [i for i, piece in enumerate(pieces) if whole or piece[0] == x]

    def place_of(i, x, asker, n):
        held_ref = held_refs[i].at[asker] if whole else held_refs[i]
        return held_ref.at[:, n]

    def columns(i):
        _, first, count = pieces[i]
        return pl.ds(first * HD, count * HD)

    def loads(x, asker):
        for n in range(capacity):
            for i in parts_of(x):
                yield pltpu.make_async_copy(
                    own_ref.at[wanted_ref[asker, 0, n], :, :, columns(i)],
                    place_of(i, x, asker, n),
                    load_sem.at[0 if whole else x],
                )

    def copy(x, asker):
        for n in range(capacity, 2 * capacity):
            page_ref = mate_ref.at[wanted_ref[asker, 0, n]]
            for i in parts_of(x):
                place_of(i, x, asker, n)[...] = page_ref[:, :, columns(i)]

    def store(i):
        return pltpu.make_async_copy(held_refs[i], out_refs[i], store_sem.at[i])

    if whole:

        @pl.loop(0, chips)
        def _(x):
            for load in loads(None, x):
                load.start()
            copy(None, x)
            for load in loads(None, x):
                load.wait()

        for i in range(len(pieces)):
            store(i).start()
    else:
        for x in places:
            for load in loads(x, mine_ref[0] ^ x):
                load.start()
        for x in places:
            copy(x, mine_ref[0] ^ x)
            for i in parts_of(x):
                half = held_refs[i].at[:, pl.ds(0, capacity)]
                pltpu.make_async_copy(half, half, load_sem.at[x]).wait()
            for i in parts_of(x):
                store(i).start()
    for i in range(len(pieces)):
        store(i).wait()


def gather_pages(mine, wanted, own, mate, pieces):
    chips = wanted.shape[0]
    shapes = []
    for x, _, count in pieces:
        shape = (2, MP // chips, PAGE, count * HD)
        shapes.append((chips,) + shape if x is None else shape)
    return pl.pallas_call(
        functools.partial(gather_kernel, pieces=tuple(pieces)),
        out_shape=[pltpu.HBM(shape, own.dtype) for shape in shapes],
        in_specs=[
            pl.BlockSpec(memory_space=pltpu.SMEM),
            pl.BlockSpec(memory_space=pltpu.SMEM),
            pl.BlockSpec(memory_space=pltpu.HBM),
            pl.BlockSpec(memory_space=pltpu.VMEM),
        ],
        out_specs=[pl.BlockSpec(memory_space=pltpu.HBM)] * len(pieces),
        scratch_shapes=[pltpu.VMEM(shape, own.dtype) for shape in shapes]
        + [
            pltpu.SemaphoreType.DMA((chips,)),
            pltpu.SemaphoreType.DMA((len(shapes),)),
        ],
        compiler_params=pltpu.CompilerParams(vmem_limit_bytes=24 * 2**20),
        cost_estimate=pl.CostEstimate(
            flops=0, bytes_accessed=2 * own.size * 2, transcendentals=0
        ),
        name="gather_pages",
    )(mine, wanted, own, mate)


def hold_back(pieces, after):
    anywhere = pl.BlockSpec(memory_space=pl.ANY)
    return pl.pallas_call(
        lambda *refs: None,
        out_shape=[pltpu.HBM(p.shape, p.dtype) for p in pieces],
        in_specs=[pl.BlockSpec(memory_space=pltpu.HBM)] * len(pieces)
        + [anywhere] * len(after),
        out_specs=[pl.BlockSpec(memory_space=pltpu.HBM)] * len(pieces),
        input_output_aliases={i: i for i in range(len(pieces))},
        name="hold_back",
    )(*pieces, *after)


def attend_kernel(*refs, first, count, starts, rows, fresh, earlier, last):
    filled_ref, live_ref, q_ref, fk_ref, fv_ref = refs[:5]
    piece_refs = refs[5 : 5 + len(starts)]
    rest = refs[5 + len(starts) :]
    if earlier:
        old_ref, old_top_ref, old_sum_ref = rest[:3]
    k_ref, v_ref = rest[-2:]
    if last:
        out_ref, held_ref, sem = rest[-5:-2]
    else:
        o_ref, top_ref, sum_ref = rest[-5:-2]
    scale = HD**-0.5 * LOG2E
    heads = HEADS
    parts = []
    for piece_ref, start in zip(piece_refs, starts):
        if len(piece_ref.shape) == 4:
            parts += [(piece_ref.at[i], start) for i in range(piece_ref.shape[0])]
        else:
            parts.append((piece_ref, start))
    tokens = parts[0][0].shape[-2]
    cached = len(parts) * tokens
    nt = (((1,), (1,)), ((), ()))
    shape = (heads * C, C)
    token = lax.rem(lax.broadcasted_iota(jnp.int32, shape, 0), C)
    causal = lax.broadcasted_iota(jnp.int32, shape, 1) <= token
    filled = token < filled_ref[0]

    def span(start, size):
        return pl.ds(pl.multiple_of(start * HD, HD), size * HD)

    def store(h, g):
        return pltpu.make_async_copy(
            held_ref.at[:, span(h * GROUP + g, heads)],
            out_ref.at[:, span((first + h) * GROUP + g, heads)],
            sem.at[h * (GROUP // heads) + g // heads],
        )

    def one_head(h):
        head = first + h
        base = head * GROUP
        fk = fk_ref[:, span(head, 1)]
        for p, (piece_ref, start) in enumerate(parts):
            at = slice(p * tokens, (p + 1) * tokens)
            live = live_ref[rows * cached + p * tokens : rows * cached + (p + 1) * tokens]
            col = span(head - start, 1)
            k_ref[at] = jnp.where(live > 0, piece_ref[0, :, col], fk[:1])
            v_ref[at, :HD] = jnp.where(live > 0, piece_ref[1, :, col], jnp.zeros_like(live))
            v_ref[at, HD:] = live
        if fresh:
            k_ref[cached:] = fk
            v_ref[cached:, :HD] = fv_ref[:, span(head, 1)]
            v_ref[cached:, HD:] = jnp.ones_like(fk)

        def scores(g):
            q = [q_ref[:, span(base + i, 1)] for i in range(g, g + heads)]
            q = jnp.concatenate(q, axis=0)
            return lax.dot_general(q, k_ref[...], nt, preferred_element_type=jnp.float32)

        def old(ref, many):
            return jnp.concatenate([ref[:, span(h * GROUP + i, 1)] for i in many], axis=0)

        ahead = scores(0)
        for g in range(0, GROUP, heads):
            many = range(g, g + heads)
            s = ahead
            if g + heads < GROUP:
                ahead = scores(g + heads)
            blocks = [s[:, i : i + HD] for i in range(0, s.shape[1], HD)]
            if fresh:
                blocks[-1] = jnp.where(causal, blocks[-1], NEG)
            top = functools.reduce(jnp.maximum, blocks)
            top = jnp.broadcast_to(jnp.max(top, axis=1, keepdims=True), top.shape)
            if earlier:
                old_top = old(old_top_ref, many)
                top = jnp.maximum(top, old_top)
            p = [jnp.exp2((b - top) * scale).astype(jnp.bfloat16) for b in blocks]
            p = jnp.concatenate(p, axis=1)
            o = jnp.dot(p, v_ref[...], preferred_element_type=jnp.float32)
            o, total = o[:, :HD], o[:, HD:]
            if earlier:
                share = jnp.exp2((old_top - top) * scale)
                o = o + share * old(old_ref, many)
                total = total + share * old(old_sum_ref, many)
            if last:
                o = jnp.where(filled, o / total, 0.0).astype(held_ref.dtype)
            for k, i in enumerate(many):
                at = slice(k * C, (k + 1) * C)
                if last:
                    held_ref[:, span(h * GROUP + i, 1)] = o[at]
                else:
                    col = span(h * GROUP + i, 1)
                    o_ref[:, col] = o[at]
                    top_ref[:, col] = top[at]
                    sum_ref[:, col] = total[at]
            if last:
                store(h, g).start()

    if count == 1:
        one_head(0)
    else:
        pl.loop(0, count)(one_head)
    if last:
        for h in range(count):
            for g in range(0, GROUP, heads):
                store(h, g).wait()


def attend(first, count, filled, live, queries, fresh_k, fresh_v, pieces, rows, out=None, earlier=None, fresh=True, last=True):
    width = GROUP * HD
    tokens = sum(
        p.shape[-2] * (p.shape[0] if p.ndim == 4 else 1) for p, start in pieces
    )
    operands = [filled, live, queries, fresh_k, fresh_v] + [p for p, start in pieces]
    if earlier is not None:
        operands += earlier
    inside = pl.BlockSpec(memory_space=pltpu.VMEM)
    in_specs = [pl.BlockSpec(memory_space=pltpu.SMEM)] + [inside] * (len(operands) - 1)
    aliases = {}
    if out is not None:
        operands.append(out)
        in_specs.append(pl.BlockSpec(memory_space=pl.ANY))
        aliases = {len(operands) - 1: 0}
    keys = tokens + (C if fresh else 0)
    scratch_shapes = [
        pltpu.VMEM((keys, HD), jnp.bfloat16),
        pltpu.VMEM((keys, 2 * HD), jnp.bfloat16),
    ]
    if last:
        out_shape = pltpu.HBM((C, H * HD), jnp.bfloat16)
        out_specs = pl.BlockSpec(memory_space=pltpu.HBM)
        scratch_shapes = [
            pltpu.VMEM((C, count * width), jnp.bfloat16),
            pltpu.SemaphoreType.DMA((count * GROUP // HEADS,)),
        ] + scratch_shapes
    else:
        out_shape = [
            jax.ShapeDtypeStruct((C, count * width), jnp.float32)
        ] * 3
        out_specs = [inside] * 3
    return pl.pallas_call(
        functools.partial(
            attend_kernel,
            first=first,
            count=count,
            starts=tuple(start for p, start in pieces),
            rows=rows,
            fresh=fresh,
            earlier=earlier is not None,
            last=last,
        ),
        out_shape=out_shape,
        in_specs=in_specs,
        out_specs=out_specs,
        scratch_shapes=scratch_shapes,
        input_output_aliases=aliases,
        compiler_params=pltpu.CompilerParams(vmem_limit_bytes=16 * 2**20),
        cost_estimate=pl.CostEstimate(
            flops=4 * count * C * width * keys,
            bytes_accessed=4 * count * C * width * 2,
            transcendentals=count * C * GROUP * keys,
        ),
        name=f"attend_{first}_{rows}",
    )(*operands)


def local(queries, fresh_kv, kv_pool, page_holder, page_slot, cached_len, fresh_len):
    devices = lax.axis_size("dp")
    chips = devices // 2
    me = lax.axis_index("dp")
    flip = chips <= MOST_PERMUTES
    same_core = [[2 * i + core for i in range(chips)] for core in range(2)]
    mate_pool = lax.ppermute(kv_pool, "dp", [(i, i ^ 1) for i in range(devices)])
    asked = ask(me.reshape(1), page_holder, page_slot, chips)
    exchange = functools.partial(
        lax.all_to_all,
        axis_name="dp",
        split_axis=0,
        concat_axis=0,
        axis_index_groups=same_core,
        tiled=True,
    )
    wanted = exchange(asked)
    own_pool = pltpu.with_memory_space_constraint(kv_pool, pltpu.HBM)
    mate_pool = pltpu.with_memory_space_constraint(mate_pool, pltpu.VMEM)
    mine = (me >> 1).reshape(1)
    gather = functools.partial(gather_pages, mine, wanted, own_pool, mate_pool)
    order = (me if flip else me & 1).reshape(1)
    live = live_tokens(order, cached_len, page_holder, MP // devices)
    fresh_k, fresh_v = fresh_kv[0, :, 0], fresh_kv[0, :, 1]

    def attend_some(first, count, pieces, *args, **kwargs):
        pieces = [
            (p.reshape(p.shape[:-3] + (-1, p.shape[-1])), start) for p, start in pieces
        ]
        return attend(
            first, count, fresh_len, live, queries[0], fresh_k, fresh_v, pieces, *args, **kwargs
        )

    out = None
    if not flip:
        sent = gather([(None, first, count) for first, count in CHUNKS])
        for (first, count), piece in zip(CHUNKS, sent):
            out = attend_some(first, count, [(exchange(piece), first)], 0, out)
        return out[None]

    def swap(piece, x):
        return lax.ppermute(piece, "dp", [(i, i ^ 2 * x) for i in range(devices)])

    near, far = range(chips // 2), range(chips // 2, chips)
    sent = gather(
        [(x, 0, KVH) for x in near]
        + [(x, first, count) for first, count in CHUNKS for x in far]
    )
    close = [(sent[x] if x == 0 else swap(sent[x], x), 0) for x in near]
    arrived = []
    for c, (first, count) in enumerate(CHUNKS):
        batch = sent[len(near) + c * len(far) : len(near) + (c + 1) * len(far)]
        if c > 0:
            batch = hold_back(batch, arrived[:2])
        arrived = [swap(piece, x) for piece, x in zip(batch, far)]
        pieces = [(piece, first) for piece in arrived]
        if c < len(CHUNKS) - 1:
            out = attend_some(first, count, close + pieces, 0, out)
        else:
            earlier = attend_some(first, count, close, 0, last=False)
            out = attend_some(
                first, count, pieces, 1, out, earlier=earlier, fresh=False
            )
    return out[None]


def solution(mesh):
    return jax.shard_map(
        local,
        mesh=mesh,
        in_specs=(
            P(("groups", "dp"), None, None),
            P(("groups", "dp"), None, None, None),
            P(("groups", "dp"), None, None, None),
            P(("groups", "dp"), None),
            P(("groups", "dp"), None),
            P(("groups", "dp")),
            P(("groups", "dp")),
        ),
        out_specs=P(("groups", "dp"), None, None),
        check_vma=False,
    )
```

```python
import functools

import jax
import jax.numpy as jnp
from jax import lax
from jax.experimental import pallas as pl
from jax.experimental.pallas import tpu as pltpu
from jax.sharding import PartitionSpec as P

H = 64
KVH = 4
HD = 128
PAGE = 8
MP = 128
C = 128
GROUP = H // KVH
LOG2E = 1.4426950408889634
NEG = -1e30
HEADS = 4
CHUNKS = ((0, 2), (2, 2))
MOST_PERMUTES = 8


def ask_kernel(me_ref, holder_ref, slot_ref, asked_ref):
    chips = asked_ref.shape[0]
    capacity = MP // (2 * chips)
    core = me_ref[0] & 1
    square = (MP, MP)
    row = lax.broadcasted_iota(jnp.int32, square, 0)
    lane = lax.broadcasted_iota(jnp.int32, square, 1)
    holder = jnp.broadcast_to(holder_ref[...], square)
    same = (holder.T == holder) & (row < lane)
    rank = jnp.sum(same.astype(jnp.int32), axis=0, keepdims=True)
    low = (holder_ref[...] & 1 ^ core) * capacity + rank
    packed = jnp.broadcast_to(low * MP + slot_ref[...], square).T
    slots = jnp.where(packed // MP == lane, packed % MP, 0)
    chip = lax.broadcasted_iota(jnp.int32, (chips, MP), 0)
    of_chip = jnp.broadcast_to(holder_ref[...] >> 1, (chips, MP)) == chip
    asked = jnp.dot(
        of_chip.astype(jnp.float32).astype(jnp.bfloat16),
        slots.astype(jnp.float32).astype(jnp.bfloat16),
        preferred_element_type=jnp.float32,
    )
    asked_ref[...] = asked.astype(jnp.int32).reshape(chips, 1, MP)


def ask(me, page_holder, page_slot, chips):
    return pl.pallas_call(
        ask_kernel,
        out_shape=jax.ShapeDtypeStruct((chips, 1, MP), jnp.int32),
        in_specs=[
            pl.BlockSpec(memory_space=pltpu.SMEM),
            pl.BlockSpec(memory_space=pltpu.VMEM),
            pl.BlockSpec(memory_space=pltpu.VMEM),
        ],
        out_specs=pl.BlockSpec(memory_space=pltpu.VMEM),
        name="ask",
    )(me, page_holder, page_slot)


def live_kernel(order_ref, length_ref, holder_ref, live_ref, *, capacity):
    square = (MP, MP)
    row = lax.broadcasted_iota(jnp.int32, square, 0)
    lane = lax.broadcasted_iota(jnp.int32, square, 1)
    holder = jnp.broadcast_to(holder_ref[...], square)
    same = (holder.T == holder) & (row < lane)
    rank = jnp.sum(same.astype(jnp.int32), axis=0, keepdims=True)
    place = (holder_ref[...] ^ order_ref[0]) * capacity + rank
    hits = jnp.broadcast_to(place, square) == row
    page = jnp.sum(jnp.where(hits, lane, 0), axis=1, keepdims=True)
    page = jnp.broadcast_to(page, square)
    shape = (MP, PAGE, HD)
    token = page[:, None, :] * PAGE + lax.broadcasted_iota(jnp.int32, shape, 1)
    live = jnp.where(token < length_ref[0], 1.0, 0.0)
    live_ref[...] = live.reshape(MP * PAGE, HD).astype(live_ref.dtype)


def live_tokens(order, cached_len, page_holder, capacity):
    return pl.pallas_call(
        functools.partial(live_kernel, capacity=capacity),
        out_shape=pltpu.VMEM((MP * PAGE, HD), jnp.bfloat16),
        in_specs=[
            pl.BlockSpec(memory_space=pltpu.SMEM),
            pl.BlockSpec(memory_space=pltpu.SMEM),
            pl.BlockSpec(memory_space=pltpu.VMEM),
        ],
        out_specs=pl.BlockSpec(memory_space=pltpu.VMEM),
        name="live_tokens",
    )(order, cached_len, page_holder)


def gather_kernel(mine_ref, wanted_ref, own_ref, mate_ref, *rest, pieces):
    out_refs = rest[: len(pieces)]
    held_ref, load_sem, store_sem = rest[len(pieces) :]
    chips, _, pages = held_ref.shape[:3]
    capacity = pages // 2
    whole = pieces[0][0] is None

    def start_loads(x, asker):
        for n in range(capacity):
            slot = wanted_ref[asker, 0, n]
            place = held_ref.at[x, :, n]
            pltpu.make_async_copy(own_ref.at[slot], place, load_sem.at[x]).start()

    def fill(x, asker):
        for n in range(capacity, pages):
            held_ref[x, :, n] = mate_ref[wanted_ref[asker, 0, n]]
        loaded = held_ref.at[x, :, pl.ds(0, capacity)]
        pltpu.make_async_copy(loaded, loaded, load_sem.at[x]).wait()

    def store(i):
        x, first, count = pieces[i]
        held = held_ref if whole else held_ref.at[x]
        lead = (slice(None),) * (len(held.shape) - 1)
        held = held.at[lead + (pl.ds(first * HD, count * HD),)]
        return pltpu.make_async_copy(held, out_refs[i], store_sem.at[i])

    if whole:

        @pl.loop(0, chips)
        def _(x):
            start_loads(x, x)
            fill(x, x)

        for i in range(len(pieces)):
            store(i).start()
    else:
        for x in reversed(range(chips)):
            start_loads(x, mine_ref[0] ^ x)
        for x in reversed(range(chips)):
            fill(x, mine_ref[0] ^ x)
            for i, piece in enumerate(pieces):
                if piece[0] == x:
                    store(i).start()
    for i in range(len(pieces)):
        store(i).wait()


def gather_pages(mine, wanted, own, mate, pieces):
    chips = wanted.shape[0]
    shapes = []
    for x, _, count in pieces:
        shape = (2, MP // chips, PAGE, count * HD)
        shapes.append((chips,) + shape if x is None else shape)
    return pl.pallas_call(
        functools.partial(gather_kernel, pieces=tuple(pieces)),
        out_shape=[pltpu.HBM(shape, own.dtype) for shape in shapes],
        in_specs=[
            pl.BlockSpec(memory_space=pltpu.SMEM),
            pl.BlockSpec(memory_space=pltpu.SMEM),
            pl.BlockSpec(memory_space=pltpu.HBM),
            pl.BlockSpec(memory_space=pltpu.VMEM),
        ],
        out_specs=[pl.BlockSpec(memory_space=pltpu.HBM)] * len(pieces),
        scratch_shapes=[
            pltpu.VMEM((chips, 2, MP // chips) + own.shape[2:], own.dtype),
            pltpu.SemaphoreType.DMA((chips,)),
            pltpu.SemaphoreType.DMA((len(shapes),)),
        ],
        compiler_params=pltpu.CompilerParams(vmem_limit_bytes=24 * 2**20),
        cost_estimate=pl.CostEstimate(
            flops=0, bytes_accessed=2 * own.size * 2, transcendentals=0
        ),
        name="gather_pages",
    )(mine, wanted, own, mate)


def hold_back(pieces, after):
    anywhere = pl.BlockSpec(memory_space=pl.ANY)
    return pl.pallas_call(
        lambda *refs: None,
        out_shape=[pltpu.HBM(p.shape, p.dtype) for p in pieces],
        in_specs=[pl.BlockSpec(memory_space=pltpu.HBM)] * len(pieces)
        + [anywhere] * len(after),
        out_specs=[pl.BlockSpec(memory_space=pltpu.HBM)] * len(pieces),
        input_output_aliases={i: i for i in range(len(pieces))},
        name="hold_back",
    )(*pieces, *after)


def attend_kernel(*refs, first, count, starts, rows, fresh, earlier, last, fetch):
    filled_ref, live_ref, q_ref, fk_ref, fv_ref = refs[:5]
    piece_refs = refs[5 : 5 + len(starts)]
    rest = refs[5 + len(starts) :]
    if earlier:
        old_ref, old_top_ref, old_sum_ref = rest[:3]
    k_ref, v_ref = rest[-2:]
    if fetch:
        raw_ref, raw_sem = rest[-4:-2]
        rest = rest[:-2]
    if last:
        out_ref, held_ref, sem = rest[-5:-2]
    else:
        o_ref, top_ref, sum_ref = rest[-5:-2]
    scale = HD**-0.5 * LOG2E
    heads = HEADS
    parts = []
    for piece_ref, start in zip(piece_refs, starts):
        if len(piece_ref.shape) == 4:
            parts += [(piece_ref.at[i], start) for i in range(piece_ref.shape[0])]
        else:
            parts.append((piece_ref, start))
    tokens = parts[0][0].shape[-2]
    cached = len(parts) * tokens
    nt = (((1,), (1,)), ((), ()))
    shape = (heads * C, C)
    token = lax.rem(lax.broadcasted_iota(jnp.int32, shape, 0), C)
    causal = lax.broadcasted_iota(jnp.int32, shape, 1) <= token
    filled = token < filled_ref[0]

    def span(start, size):
        return pl.ds(pl.multiple_of(start * HD, HD), size * HD)

    def store(h, g):
        return pltpu.make_async_copy(
            held_ref.at[:, span(h * GROUP + g, heads)],
            out_ref.at[:, span((first + h) * GROUP + g, heads)],
            sem.at[h * (GROUP // heads) + g // heads],
        )

    def load(p):
        piece_ref, start = parts[p]
        cols = pl.ds((first - start) * HD, count * HD)
        return pltpu.make_async_copy(
            piece_ref.at[:, :, cols], raw_ref.at[p], raw_sem.at[p]
        )

    if fetch:
        for p in range(len(parts)):
            load(p).start()
        for p in range(len(parts)):
            load(p).wait()

    def part(p, kind, h):
        if fetch:
            return raw_ref[p, kind, :, span(h, 1)]
        piece_ref, start = parts[p]
        return piece_ref[kind, :, span(first + h - start, 1)]

    def one_head(h):
        head = first + h
        base = head * GROUP
        fk = fk_ref[:, span(head, 1)]
        for p in range(len(parts)):
            at = slice(p * tokens, (p + 1) * tokens)
            live = live_ref[rows * cached + p * tokens : rows * cached + (p + 1) * tokens]
            k_ref[at] = jnp.where(live > 0, part(p, 0, h), fk[:1])
            v_ref[at, :HD] = jnp.where(live > 0, part(p, 1, h), jnp.zeros_like(live))
            v_ref[at, HD:] = live
        if fresh:
            k_ref[cached:] = fk
            v_ref[cached:, :HD] = fv_ref[:, span(head, 1)]
            v_ref[cached:, HD:] = jnp.ones_like(fk)

        def scores(g):
            q = [q_ref[:, span(base + i, 1)] for i in range(g, g + heads)]
            q = jnp.concatenate(q, axis=0)
            return lax.dot_general(q, k_ref[...], nt, preferred_element_type=jnp.float32)

        def old(ref, many):
            return jnp.concatenate([ref[:, span(h * GROUP + i, 1)] for i in many], axis=0)

        ahead = scores(0)
        for g in range(0, GROUP, heads):
            many = range(g, g + heads)
            s = ahead
            if g + heads < GROUP:
                ahead = scores(g + heads)
            blocks = [s[:, i : i + HD] for i in range(0, s.shape[1], HD)]
            if fresh:
                blocks[-1] = jnp.where(causal, blocks[-1], NEG)
            top = functools.reduce(jnp.maximum, blocks)
            top = jnp.broadcast_to(jnp.max(top, axis=1, keepdims=True), top.shape)
            if earlier:
                old_top = old(old_top_ref, many)
                top = jnp.maximum(top, old_top)
            p = [jnp.exp2((b - top) * scale).astype(jnp.bfloat16) for b in blocks]
            p = jnp.concatenate(p, axis=1)
            o = jnp.dot(p, v_ref[...], preferred_element_type=jnp.float32)
            o, total = o[:, :HD], o[:, HD:]
            if earlier:
                share = jnp.exp2((old_top - top) * scale)
                o = o + share * old(old_ref, many)
                total = total + share * old(old_sum_ref, many)
            if last:
                o = jnp.where(filled, o / total, 0.0).astype(held_ref.dtype)
            for k, i in enumerate(many):
                at = slice(k * C, (k + 1) * C)
                if last:
                    held_ref[:, span(h * GROUP + i, 1)] = o[at]
                else:
                    col = span(h * GROUP + i, 1)
                    o_ref[:, col] = o[at]
                    top_ref[:, col] = top[at]
                    sum_ref[:, col] = total[at]
            if last:
                store(h, g).start()

    if count == 1:
        one_head(0)
    else:
        pl.loop(0, count)(one_head)
    if last:
        for h in range(count):
            for g in range(0, GROUP, heads):
                store(h, g).wait()


def attend(first, count, filled, live, queries, fresh_k, fresh_v, pieces, rows, out=None, earlier=None, fresh=True, last=True, fetch=True):
    width = GROUP * HD
    tokens = sum(
        p.shape[-2] * (p.shape[0] if p.ndim == 4 else 1) for p, start in pieces
    )
    operands = [filled, live, queries, fresh_k, fresh_v]
    operands += [
        pltpu.with_memory_space_constraint(p, pltpu.HBM) if fetch else p
        for p, start in pieces
    ]
    if earlier is not None:
        operands += earlier
    inside = pl.BlockSpec(memory_space=pltpu.VMEM)
    outside = pl.BlockSpec(memory_space=pltpu.HBM)
    in_specs = [pl.BlockSpec(memory_space=pltpu.SMEM)] + [inside] * (len(operands) - 1)
    if fetch:
        in_specs[5 : 5 + len(pieces)] = [outside] * len(pieces)
    aliases = {}
    if out is not None:
        operands.append(out)
        in_specs.append(pl.BlockSpec(memory_space=pl.ANY))
        aliases = {len(operands) - 1: 0}
    keys = tokens + (C if fresh else 0)
    each = pieces[0][0].shape[-2]
    scratch_shapes = [
        pltpu.VMEM((keys, HD), jnp.bfloat16),
        pltpu.VMEM((keys, 2 * HD), jnp.bfloat16),
    ]
    if fetch:
        scratch_shapes = [
            pltpu.VMEM((tokens // each, 2, each, count * HD), jnp.bfloat16),
            pltpu.SemaphoreType.DMA((tokens // each,)),
        ] + scratch_shapes
    if last:
        out_shape = pltpu.HBM((C, H * HD), jnp.bfloat16)
        out_specs = pl.BlockSpec(memory_space=pltpu.HBM)
        scratch_shapes = [
            pltpu.VMEM((C, count * width), jnp.bfloat16),
            pltpu.SemaphoreType.DMA((count * GROUP // HEADS,)),
        ] + scratch_shapes
    else:
        out_shape = [
            jax.ShapeDtypeStruct((C, count * width), jnp.float32)
        ] * 3
        out_specs = [inside] * 3
    return pl.pallas_call(
        functools.partial(
            attend_kernel,
            first=first,
            count=count,
            starts=tuple(start for p, start in pieces),
            rows=rows,
            fresh=fresh,
            earlier=earlier is not None,
            last=last,
            fetch=fetch,
        ),
        out_shape=out_shape,
        in_specs=in_specs,
        out_specs=out_specs,
        scratch_shapes=scratch_shapes,
        input_output_aliases=aliases,
        compiler_params=pltpu.CompilerParams(vmem_limit_bytes=16 * 2**20),
        cost_estimate=pl.CostEstimate(
            flops=4 * count * C * width * keys,
            bytes_accessed=4 * count * C * width * 2,
            transcendentals=count * C * GROUP * keys,
        ),
        name=f"attend_{first}_{rows}",
    )(*operands)


def local(queries, fresh_kv, kv_pool, page_holder, page_slot, cached_len, fresh_len):
    devices = lax.axis_size("dp")
    chips = devices // 2
    me = lax.axis_index("dp")
    flip = chips <= MOST_PERMUTES
    same_core = [[2 * i + core for i in range(chips)] for core in range(2)]
    mate_pool = lax.ppermute(kv_pool, "dp", [(i, i ^ 1) for i in range(devices)])
    asked = ask(me.reshape(1), page_holder, page_slot, chips)
    exchange = functools.partial(
        lax.all_to_all,
        axis_name="dp",
        split_axis=0,
        concat_axis=0,
        axis_index_groups=same_core,
        tiled=True,
    )
    wanted = exchange(asked)
    own_pool = pltpu.with_memory_space_constraint(kv_pool, pltpu.HBM)
    mate_pool = pltpu.with_memory_space_constraint(mate_pool, pltpu.VMEM)
    mine = (me >> 1).reshape(1)
    gather = functools.partial(gather_pages, mine, wanted, own_pool, mate_pool)
    order = (me if flip else me & 1).reshape(1)
    live = live_tokens(order, cached_len, page_holder, MP // devices)
    fresh_k, fresh_v = fresh_kv[0, :, 0], fresh_kv[0, :, 1]

    def attend_some(first, count, pieces, *args, **kwargs):
        pieces = [
            (p.reshape(p.shape[:-3] + (-1, p.shape[-1])), start) for p, start in pieces
        ]
        return attend(
            first, count, fresh_len, live, queries[0], fresh_k, fresh_v, pieces, *args, **kwargs
        )

    out = None
    if not flip:
        sent = gather([(None, first, count) for first, count in CHUNKS])
        for (first, count), piece in zip(CHUNKS, sent):
            out = attend_some(first, count, [(exchange(piece), first)], 0, out)
        return out[None]

    def swap(piece, x):
        return lax.ppermute(piece, "dp", [(i, i ^ 2 * x) for i in range(devices)])

    near, far = range(chips // 2), range(chips // 2, chips)
    sent = gather(
        [(x, 0, KVH) for x in near]
        + [(x, first, count) for first, count in CHUNKS for x in far]
    )
    close = [(sent[x] if x == 0 else swap(sent[x], x), 0) for x in near]
    arrived = []
    for c, (first, count) in enumerate(CHUNKS):
        batch = sent[len(near) + c * len(far) : len(near) + (c + 1) * len(far)]
        if c > 0:
            batch = hold_back(batch, arrived[:2])
        arrived = [swap(piece, x) for piece, x in zip(batch, far)]
        pieces = [(piece, first) for piece in arrived]
        if c < len(CHUNKS) - 1:
            out = attend_some(first, count, close + pieces, 0, out)
        else:
            earlier = attend_some(first, count, close, 0, last=False)
            out = attend_some(
                first, count, pieces, 1, out, earlier=earlier, fresh=False, fetch=False
            )
    return out[None]


def solution(mesh):
    return jax.shard_map(
        local,
        mesh=mesh,
        in_specs=(
            P(("groups", "dp"), None, None),
            P(("groups", "dp"), None, None, None),
            P(("groups", "dp"), None, None, None),
            P(("groups", "dp"), None),
            P(("groups", "dp"), None),
            P(("groups", "dp")),
            P(("groups", "dp")),
        ),
        out_specs=P(("groups", "dp"), None, None),
        check_vma=False,
    )
```

```python
import functools

import jax
import jax.numpy as jnp
from jax import lax
from jax.experimental import pallas as pl
from jax.experimental.pallas import tpu as pltpu
from jax.sharding import PartitionSpec as P

H = 64
KVH = 4
HD = 128
PAGE = 8
MP = 128
C = 128
GROUP = H // KVH
LOG2E = 1.4426950408889634
NEG = -1e30
HEADS = 4
CHUNKS = ((0, 2), (2, 2))
MOST_PERMUTES = 8


def ask_kernel(me_ref, holder_ref, slot_ref, asked_ref):
    chips = asked_ref.shape[0]
    capacity = MP // (2 * chips)
    core = me_ref[0] & 1
    square = (MP, MP)
    row = lax.broadcasted_iota(jnp.int32, square, 0)
    lane = lax.broadcasted_iota(jnp.int32, square, 1)
    holder = jnp.broadcast_to(holder_ref[...], square)
    same = (holder.T == holder) & (row < lane)
    rank = jnp.sum(same.astype(jnp.int32), axis=0, keepdims=True)
    low = (holder_ref[...] & 1 ^ core) * capacity + rank
    packed = jnp.broadcast_to(low * MP + slot_ref[...], square).T
    slots = jnp.where(packed // MP == lane, packed % MP, 0)
    chip = lax.broadcasted_iota(jnp.int32, (chips, MP), 0)
    of_chip = jnp.broadcast_to(holder_ref[...] >> 1, (chips, MP)) == chip
    asked = jnp.dot(
        of_chip.astype(jnp.float32).astype(jnp.bfloat16),
        slots.astype(jnp.float32).astype(jnp.bfloat16),
        preferred_element_type=jnp.float32,
    )
    asked_ref[...] = asked.astype(jnp.int32).reshape(chips, 1, MP)


def ask(me, page_holder, page_slot, chips):
    return pl.pallas_call(
        ask_kernel,
        out_shape=jax.ShapeDtypeStruct((chips, 1, MP), jnp.int32),
        in_specs=[
            pl.BlockSpec(memory_space=pltpu.SMEM),
            pl.BlockSpec(memory_space=pltpu.VMEM),
            pl.BlockSpec(memory_space=pltpu.VMEM),
        ],
        out_specs=pl.BlockSpec(memory_space=pltpu.VMEM),
        name="ask",
    )(me, page_holder, page_slot)


def live_kernel(order_ref, length_ref, holder_ref, live_ref, *, capacity):
    square = (MP, MP)
    row = lax.broadcasted_iota(jnp.int32, square, 0)
    lane = lax.broadcasted_iota(jnp.int32, square, 1)
    holder = jnp.broadcast_to(holder_ref[...], square)
    same = (holder.T == holder) & (row < lane)
    rank = jnp.sum(same.astype(jnp.int32), axis=0, keepdims=True)
    place = (holder_ref[...] ^ order_ref[0]) * capacity + rank
    hits = jnp.broadcast_to(place, square) == row
    page = jnp.sum(jnp.where(hits, lane, 0), axis=1, keepdims=True)
    page = jnp.broadcast_to(page, square)
    shape = (MP, PAGE, HD)
    token = page[:, None, :] * PAGE + lax.broadcasted_iota(jnp.int32, shape, 1)
    live = jnp.where(token < length_ref[0], 1.0, 0.0)
    live_ref[...] = live.reshape(MP * PAGE, HD).astype(live_ref.dtype)


def live_tokens(order, cached_len, page_holder, capacity):
    return pl.pallas_call(
        functools.partial(live_kernel, capacity=capacity),
        out_shape=pltpu.VMEM((MP * PAGE, HD), jnp.bfloat16),
        in_specs=[
            pl.BlockSpec(memory_space=pltpu.SMEM),
            pl.BlockSpec(memory_space=pltpu.SMEM),
            pl.BlockSpec(memory_space=pltpu.VMEM),
        ],
        out_specs=pl.BlockSpec(memory_space=pltpu.VMEM),
        name="live_tokens",
    )(order, cached_len, page_holder)


def gather_kernel(mine_ref, wanted_ref, own_ref, mate_ref, *rest, pieces):
    out_refs = rest[: len(pieces)]
    held_ref, load_sem, store_sem = rest[len(pieces) :]
    chips, _, pages = held_ref.shape[:3]
    capacity = pages // 2
    whole = pieces[0][0] is None

    def start_loads(x, asker):
        for n in range(capacity):
            slot = wanted_ref[asker, 0, n]
            place = held_ref.at[x, :, n]
            pltpu.make_async_copy(own_ref.at[slot], place, load_sem.at[x]).start()

    def fill(x, asker):
        for n in range(capacity, pages):
            held_ref[x, :, n] = mate_ref[wanted_ref[asker, 0, n]]
        loaded = held_ref.at[x, :, pl.ds(0, capacity)]
        pltpu.make_async_copy(loaded, loaded, load_sem.at[x]).wait()

    def store(i):
        x, first, count = pieces[i]
        held = held_ref if whole else held_ref.at[x]
        lead = (slice(None),) * (len(held.shape) - 1)
        held = held.at[lead + (pl.ds(first * HD, count * HD),)]
        return pltpu.make_async_copy(held, out_refs[i], store_sem.at[i])

    if whole:

        @pl.loop(0, chips)
        def _(x):
            start_loads(x, x)
            fill(x, x)

        for i in range(len(pieces)):
            store(i).start()
    else:
        for x in reversed(range(chips)):
            start_loads(x, mine_ref[0] ^ x)
        for x in reversed(range(chips)):
            fill(x, mine_ref[0] ^ x)
            for i, piece in enumerate(pieces):
                if piece[0] == x:
                    store(i).start()
    for i in range(len(pieces)):
        store(i).wait()


def gather_pages(mine, wanted, own, mate, pieces):
    chips = wanted.shape[0]
    shapes = []
    for x, _, count in pieces:
        shape = (2, MP // chips, PAGE, count * HD)
        shapes.append((chips,) + shape if x is None else shape)
    spaces = [
        pltpu.VMEM if x is not None and (0 < x < chips // 2 or (first == 0 and 0 <= x - chips // 2 < 2)) else pltpu.HBM
        for x, first, _ in pieces
    ]
    return pl.pallas_call(
        functools.partial(gather_kernel, pieces=tuple(pieces)),
        out_shape=[space(shape, own.dtype) for space, shape in zip(spaces, shapes)],
        in_specs=[
            pl.BlockSpec(memory_space=pltpu.SMEM),
            pl.BlockSpec(memory_space=pltpu.SMEM),
            pl.BlockSpec(memory_space=pltpu.HBM),
            pl.BlockSpec(memory_space=pltpu.VMEM),
        ],
        out_specs=[pl.BlockSpec(memory_space=space) for space in spaces],
        scratch_shapes=[
            pltpu.VMEM((chips, 2, MP // chips) + own.shape[2:], own.dtype),
            pltpu.SemaphoreType.DMA((chips,)),
            pltpu.SemaphoreType.DMA((len(shapes),)),
        ],
        compiler_params=pltpu.CompilerParams(vmem_limit_bytes=24 * 2**20),
        cost_estimate=pl.CostEstimate(
            flops=0, bytes_accessed=2 * own.size * 2, transcendentals=0
        ),
        name="gather_pages",
    )(mine, wanted, own, mate)


def hold_back(pieces, after):
    anywhere = pl.BlockSpec(memory_space=pl.ANY)
    return pl.pallas_call(
        lambda *refs: None,
        out_shape=[pltpu.HBM(p.shape, p.dtype) for p in pieces],
        in_specs=[pl.BlockSpec(memory_space=pltpu.HBM)] * len(pieces)
        + [anywhere] * len(after),
        out_specs=[pl.BlockSpec(memory_space=pltpu.HBM)] * len(pieces),
        input_output_aliases={i: i for i in range(len(pieces))},
        name="hold_back",
    )(*pieces, *after)


def attend_kernel(*refs, first, count, starts, rows, fresh, earlier, last, fetch):
    filled_ref, live_ref, q_ref, fk_ref, fv_ref = refs[:5]
    piece_refs = refs[5 : 5 + len(starts)]
    rest = refs[5 + len(starts) :]
    if earlier:
        old_ref, old_top_ref, old_sum_ref = rest[:3]
    k_ref, v_ref = rest[-2:]
    if fetch:
        raw_ref, raw_sem = rest[-4:-2]
        rest = rest[:-2]
    if last:
        out_ref, held_ref, sem = rest[-5:-2]
    else:
        o_ref, top_ref, sum_ref = rest[-5:-2]
    scale = HD**-0.5 * LOG2E
    heads = HEADS
    parts = []
    for piece_ref, start in zip(piece_refs, starts):
        if len(piece_ref.shape) == 4:
            parts += [(piece_ref.at[i], start) for i in range(piece_ref.shape[0])]
        else:
            parts.append((piece_ref, start))
    tokens = parts[0][0].shape[-2]
    cached = len(parts) * tokens
    nt = (((1,), (1,)), ((), ()))
    shape = (heads * C, C)
    token = lax.rem(lax.broadcasted_iota(jnp.int32, shape, 0), C)
    causal = lax.broadcasted_iota(jnp.int32, shape, 1) <= token
    filled = token < filled_ref[0]

    def span(start, size):
        return pl.ds(start * HD, size * HD)

    def store(h, g):
        return pltpu.make_async_copy(
            held_ref.at[:, span(h * GROUP + g, heads)],
            out_ref.at[:, span((first + h) * GROUP + g, heads)],
            sem.at[h * (GROUP // heads) + g // heads],
        )

    def load(p):
        piece_ref, start = parts[p]
        cols = pl.ds((first - start) * HD, count * HD)
        return pltpu.make_async_copy(
            piece_ref.at[:, :, cols], raw_ref.at[p], raw_sem.at[p]
        )

    if fetch:
        for p in range(len(parts)):
            load(p).start()

    def part(p, kind, h):
        if fetch:
            return raw_ref[p, kind, :, span(h, 1)]
        piece_ref, start = parts[p]
        return piece_ref[kind, :, span(first + h - start, 1)]

    def one_head(h):
        head = first + h
        base = head * GROUP
        fk = fk_ref[:, span(head, 1)]
        for p in range(len(parts)):
            at = slice(p * tokens, (p + 1) * tokens)
            if fetch and h == 0:
                load(p).wait()
            live = live_ref[rows * cached + p * tokens : rows * cached + (p + 1) * tokens]
            k_ref[at] = jnp.where(live > 0, part(p, 0, h), fk[:1])
            v_ref[at, :HD] = jnp.where(live > 0, part(p, 1, h), jnp.zeros_like(live))
            v_ref[at, HD:] = live
        if fresh:
            k_ref[cached:] = fk
            v_ref[cached:, :HD] = fv_ref[:, span(head, 1)]
            v_ref[cached:, HD:] = jnp.ones_like(fk)

        def scores(g):
            q = [q_ref[:, span(base + i, 1)] for i in range(g, g + heads)]
            q = jnp.concatenate(q, axis=0)
            return lax.dot_general(q, k_ref[...], nt, preferred_element_type=jnp.float32)

        def old(ref, many):
            return jnp.concatenate([ref[:, span(h * GROUP + i, 1)] for i in many], axis=0)

        ahead = scores(0)
        for g in range(0, GROUP, heads):
            many = range(g, g + heads)
            s = ahead
            if g + heads < GROUP:
                ahead = scores(g + heads)
            blocks = [s[:, i : i + HD] for i in range(0, s.shape[1], HD)]
            if fresh:
                blocks[-1] = jnp.where(causal, blocks[-1], NEG)
            top = functools.reduce(jnp.maximum, blocks)
            top = jnp.broadcast_to(jnp.max(top, axis=1, keepdims=True), top.shape)
            if earlier:
                old_top = old(old_top_ref, many)
                top = jnp.maximum(top, old_top)
            p = [jnp.exp2((b - top) * scale).astype(jnp.bfloat16) for b in blocks]
            p = jnp.concatenate(p, axis=1)
            o = jnp.dot(p, v_ref[...], preferred_element_type=jnp.float32)
            o, total = o[:, :HD], o[:, HD:]
            if earlier:
                share = jnp.exp2((old_top - top) * scale)
                o = o + share * old(old_ref, many)
                total = total + share * old(old_sum_ref, many)
            if last:
                o = jnp.where(filled, o / total, 0.0).astype(held_ref.dtype)
            for k, i in enumerate(many):
                at = slice(k * C, (k + 1) * C)
                if last:
                    held_ref[:, span(h * GROUP + i, 1)] = o[at]
                else:
                    col = span(h * GROUP + i, 1)
                    o_ref[:, col] = o[at]
                    top_ref[:, col] = top[at]
                    sum_ref[:, col] = total[at]
            if last:
                store(h, g).start()

    for h in range(count):
        one_head(h)
    if last:
        for h in range(count):
            for g in range(0, GROUP, heads):
                store(h, g).wait()


def attend(first, count, filled, live, queries, fresh_k, fresh_v, pieces, rows, out=None, earlier=None, fresh=True, last=True, fetch=True):
    width = GROUP * HD
    tokens = sum(
        p.shape[-2] * (p.shape[0] if p.ndim == 4 else 1) for p, start in pieces
    )
    operands = [filled, live, queries, fresh_k, fresh_v]
    operands += [
        pltpu.with_memory_space_constraint(p, pltpu.HBM) if fetch else p
        for p, start in pieces
    ]
    if earlier is not None:
        operands += earlier
    inside = pl.BlockSpec(memory_space=pltpu.VMEM)
    outside = pl.BlockSpec(memory_space=pltpu.HBM)
    in_specs = [pl.BlockSpec(memory_space=pltpu.SMEM)] + [inside] * (len(operands) - 1)
    if fetch:
        in_specs[5 : 5 + len(pieces)] = [outside] * len(pieces)
    aliases = {}
    if out is not None:
        operands.append(out)
        in_specs.append(pl.BlockSpec(memory_space=pl.ANY))
        aliases = {len(operands) - 1: 0}
    keys = tokens + (C if fresh else 0)
    each = pieces[0][0].shape[-2]
    scratch_shapes = [
        pltpu.VMEM((keys, HD), jnp.bfloat16),
        pltpu.VMEM((keys, 2 * HD), jnp.bfloat16),
    ]
    if fetch:
        scratch_shapes = [
            pltpu.VMEM((tokens // each, 2, each, count * HD), jnp.bfloat16),
            pltpu.SemaphoreType.DMA((tokens // each,)),
        ] + scratch_shapes
    if last:
        out_shape = pltpu.HBM((C, H * HD), jnp.bfloat16)
        out_specs = pl.BlockSpec(memory_space=pltpu.HBM)
        scratch_shapes = [
            pltpu.VMEM((C, count * width), jnp.bfloat16),
            pltpu.SemaphoreType.DMA((count * GROUP // HEADS,)),
        ] + scratch_shapes
    else:
        out_shape = [
            jax.ShapeDtypeStruct((C, count * width), jnp.float32)
        ] * 3
        out_specs = [inside] * 3
    return pl.pallas_call(
        functools.partial(
            attend_kernel,
            first=first,
            count=count,
            starts=tuple(start for p, start in pieces),
            rows=rows,
            fresh=fresh,
            earlier=earlier is not None,
            last=last,
            fetch=fetch,
        ),
        out_shape=out_shape,
        in_specs=in_specs,
        out_specs=out_specs,
        scratch_shapes=scratch_shapes,
        input_output_aliases=aliases,
        compiler_params=pltpu.CompilerParams(vmem_limit_bytes=16 * 2**20),
        cost_estimate=pl.CostEstimate(
            flops=4 * count * C * width * keys,
            bytes_accessed=4 * count * C * width * 2,
            transcendentals=count * C * GROUP * keys,
        ),
        name=f"attend_{first}_{rows}",
    )(*operands)


def local(queries, fresh_kv, kv_pool, page_holder, page_slot, cached_len, fresh_len):
    devices = lax.axis_size("dp")
    chips = devices // 2
    me = lax.axis_index("dp")
    flip = chips <= MOST_PERMUTES
    same_core = [[2 * i + core for i in range(chips)] for core in range(2)]
    mate_pool = lax.ppermute(kv_pool, "dp", [(i, i ^ 1) for i in range(devices)])
    asked = ask(me.reshape(1), page_holder, page_slot, chips)
    exchange = functools.partial(
        lax.all_to_all,
        axis_name="dp",
        split_axis=0,
        concat_axis=0,
        axis_index_groups=same_core,
        tiled=True,
    )
    wanted = exchange(asked)
    own_pool = pltpu.with_memory_space_constraint(kv_pool, pltpu.HBM)
    mate_pool = pltpu.with_memory_space_constraint(mate_pool, pltpu.VMEM)
    mine = (me >> 1).reshape(1)
    gather = functools.partial(gather_pages, mine, wanted, own_pool, mate_pool)
    order = (me if flip else me & 1).reshape(1)
    live = live_tokens(order, cached_len, page_holder, MP // devices)
    fresh_k, fresh_v = fresh_kv[0, :, 0], fresh_kv[0, :, 1]

    def attend_some(first, count, pieces, *args, **kwargs):
        pieces = [
            (p.reshape(p.shape[:-3] + (-1, p.shape[-1])), start) for p, start in pieces
        ]
        return attend(
            first, count, fresh_len, live, queries[0], fresh_k, fresh_v, pieces, *args, **kwargs
        )

    out = None
    if not flip:
        sent = gather([(None, first, count) for first, count in CHUNKS])
        for (first, count), piece in zip(CHUNKS, sent):
            out = attend_some(first, count, [(exchange(piece), first)], 0, out)
        return out[None]

    def swap(piece, x):
        return lax.ppermute(piece, "dp", [(i, i ^ 2 * x) for i in range(devices)])

    near, far = range(chips // 2), range(chips // 2, chips)
    sent = gather(
        [(x, 0, KVH) for x in near]
        + [(x, first, count) for first, count in CHUNKS for x in far]
    )
    close = [(sent[x] if x == 0 else swap(sent[x], x), 0) for x in near]
    arrived = []
    for c, (first, count) in enumerate(CHUNKS):
        batch = sent[len(near) + c * len(far) : len(near) + (c + 1) * len(far)]
        if c > 0:
            batch = hold_back(batch, arrived[:2])
        arrived = [swap(piece, x) for piece, x in zip(batch, far)]
        pieces = [(piece, first) for piece in arrived]
        if c < len(CHUNKS) - 1:
            out = attend_some(first, count, close + pieces, 0, out)
        else:
            earlier = attend_some(first, count, close, 0, last=False)
            out = attend_some(
                first, count, pieces, 1, out, earlier=earlier, fresh=False, fetch=False
            )
    return out[None]


def solution(mesh):
    return jax.shard_map(
        local,
        mesh=mesh,
        in_specs=(
            P(("groups", "dp"), None, None),
            P(("groups", "dp"), None, None, None),
            P(("groups", "dp"), None, None, None),
            P(("groups", "dp"), None),
            P(("groups", "dp"), None),
            P(("groups", "dp")),
            P(("groups", "dp")),
        ),
        out_specs=P(("groups", "dp"), None, None),
        check_vma=False,
    )
```

```python
import functools

import jax
import jax.numpy as jnp
from jax import lax
from jax.experimental import pallas as pl
from jax.experimental.pallas import tpu as pltpu
from jax.sharding import PartitionSpec as P

H = 64
KVH = 4
HD = 128
PAGE = 8
MP = 128
C = 128
GROUP = H // KVH
LOG2E = 1.4426950408889634
NEG = -1e30
HEADS = 4
CHUNKS = ((0, 2), (2, 2))
MOST_PERMUTES = 8


def ask_kernel(me_ref, holder_ref, slot_ref, asked_ref):
    chips = asked_ref.shape[0]
    capacity = MP // (2 * chips)
    core = me_ref[0] & 1
    square = (MP, MP)
    row = lax.broadcasted_iota(jnp.int32, square, 0)
    lane = lax.broadcasted_iota(jnp.int32, square, 1)
    holder = jnp.broadcast_to(holder_ref[...], square)
    same = (holder.T == holder) & (row < lane)
    rank = jnp.sum(same.astype(jnp.int32), axis=0, keepdims=True)
    low = (holder_ref[...] & 1 ^ core) * capacity + rank
    packed = jnp.broadcast_to(low * MP + slot_ref[...], square).T
    slots = jnp.where(packed // MP == lane, packed % MP, 0)
    chip = lax.broadcasted_iota(jnp.int32, (chips, MP), 0)
    of_chip = jnp.broadcast_to(holder_ref[...] >> 1, (chips, MP)) == chip
    asked = jnp.dot(
        of_chip.astype(jnp.float32).astype(jnp.bfloat16),
        slots.astype(jnp.float32).astype(jnp.bfloat16),
        preferred_element_type=jnp.float32,
    )
    asked_ref[...] = asked.astype(jnp.int32).reshape(chips, 1, MP)


def ask(me, page_holder, page_slot, chips):
    return pl.pallas_call(
        ask_kernel,
        out_shape=jax.ShapeDtypeStruct((chips, 1, MP), jnp.int32),
        in_specs=[
            pl.BlockSpec(memory_space=pltpu.SMEM),
            pl.BlockSpec(memory_space=pltpu.VMEM),
            pl.BlockSpec(memory_space=pltpu.VMEM),
        ],
        out_specs=pl.BlockSpec(memory_space=pltpu.VMEM),
        name="ask",
    )(me, page_holder, page_slot)


def live_kernel(order_ref, length_ref, holder_ref, live_ref, *, capacity):
    square = (MP, MP)
    row = lax.broadcasted_iota(jnp.int32, square, 0)
    lane = lax.broadcasted_iota(jnp.int32, square, 1)
    holder = jnp.broadcast_to(holder_ref[...], square)
    same = (holder.T == holder) & (row < lane)
    rank = jnp.sum(same.astype(jnp.int32), axis=0, keepdims=True)
    place = (holder_ref[...] ^ order_ref[0]) * capacity + rank
    hits = jnp.broadcast_to(place, square) == row
    page = jnp.sum(jnp.where(hits, lane, 0), axis=1, keepdims=True)
    page = jnp.broadcast_to(page, square)
    shape = (MP, PAGE, HD)
    token = page[:, None, :] * PAGE + lax.broadcasted_iota(jnp.int32, shape, 1)
    live = jnp.where(token < length_ref[0], 1.0, 0.0)
    live_ref[...] = live.reshape(MP * PAGE, HD).astype(live_ref.dtype)


def live_tokens(order, cached_len, page_holder, capacity):
    return pl.pallas_call(
        functools.partial(live_kernel, capacity=capacity),
        out_shape=pltpu.VMEM((MP * PAGE, HD), jnp.bfloat16),
        in_specs=[
            pl.BlockSpec(memory_space=pltpu.SMEM),
            pl.BlockSpec(memory_space=pltpu.SMEM),
            pl.BlockSpec(memory_space=pltpu.VMEM),
        ],
        out_specs=pl.BlockSpec(memory_space=pltpu.VMEM),
        name="live_tokens",
    )(order, cached_len, page_holder)


def gather_kernel(mine_ref, wanted_ref, own_ref, mate_ref, *rest, pieces):
    out_refs = rest[: len(pieces)]
    held_ref, load_sem, store_sem = rest[len(pieces) :]
    chips, _, pages = held_ref.shape[:3]
    capacity = pages // 2
    whole = pieces[0][0] is None

    def start_loads(x, asker):
        for n in range(capacity):
            slot = wanted_ref[asker, 0, n]
            place = held_ref.at[x, :, n]
            pltpu.make_async_copy(own_ref.at[slot], place, load_sem.at[x]).start()

    def fill(x, asker):
        for n in range(capacity, pages):
            held_ref[x, :, n] = mate_ref[wanted_ref[asker, 0, n]]
        loaded = held_ref.at[x, :, pl.ds(0, capacity)]
        pltpu.make_async_copy(loaded, loaded, load_sem.at[x]).wait()

    def store(i):
        x, first, count = pieces[i]
        held = held_ref if whole else held_ref.at[x]
        lead = (slice(None),) * (len(held.shape) - 1)
        held = held.at[lead + (pl.ds(first * HD, count * HD),)]
        return pltpu.make_async_copy(held, out_refs[i], store_sem.at[i])

    if whole:

        @pl.loop(0, chips)
        def _(x):
            start_loads(x, x)
            fill(x, x)

        for i in range(len(pieces)):
            store(i).start()
    else:
        for x in reversed(range(chips)):
            start_loads(x, mine_ref[0] ^ x)
        for x in reversed(range(chips)):
            fill(x, mine_ref[0] ^ x)
            for i, piece in enumerate(pieces):
                if piece[0] == x:
                    store(i).start()
    for i in range(len(pieces)):
        store(i).wait()


def gather_pages(mine, wanted, own, mate, pieces):
    chips = wanted.shape[0]
    shapes = []
    for x, _, count in pieces:
        shape = (2, MP // chips, PAGE, count * HD)
        shapes.append((chips,) + shape if x is None else shape)
    spaces = [
        pltpu.VMEM if x is not None and (0 < x < chips // 2 or (first == 0 and 0 <= x - chips // 2 < 2)) else pltpu.HBM
        for x, first, _ in pieces
    ]
    return pl.pallas_call(
        functools.partial(gather_kernel, pieces=tuple(pieces)),
        out_shape=[space(shape, own.dtype) for space, shape in zip(spaces, shapes)],
        in_specs=[
            pl.BlockSpec(memory_space=pltpu.SMEM),
            pl.BlockSpec(memory_space=pltpu.SMEM),
            pl.BlockSpec(memory_space=pltpu.HBM),
            pl.BlockSpec(memory_space=pltpu.VMEM),
        ],
        out_specs=[pl.BlockSpec(memory_space=space) for space in spaces],
        scratch_shapes=[
            pltpu.VMEM((chips, 2, MP // chips) + own.shape[2:], own.dtype),
            pltpu.SemaphoreType.DMA((chips,)),
            pltpu.SemaphoreType.DMA((len(shapes),)),
        ],
        compiler_params=pltpu.CompilerParams(vmem_limit_bytes=24 * 2**20),
        cost_estimate=pl.CostEstimate(
            flops=0, bytes_accessed=2 * own.size * 2, transcendentals=0
        ),
        name="gather_pages",
    )(mine, wanted, own, mate)


def hold_back(pieces, after):
    anywhere = pl.BlockSpec(memory_space=pl.ANY)
    return pl.pallas_call(
        lambda *refs: None,
        out_shape=[pltpu.HBM(p.shape, p.dtype) for p in pieces],
        in_specs=[pl.BlockSpec(memory_space=pltpu.HBM)] * len(pieces)
        + [anywhere] * len(after),
        out_specs=[pl.BlockSpec(memory_space=pltpu.HBM)] * len(pieces),
        input_output_aliases={i: i for i in range(len(pieces))},
        name="hold_back",
    )(*pieces, *after)


def attend_kernel(*refs, first, count, starts, rows, fresh, earlier, last, fetch):
    filled_ref, live_ref, q_ref, fk_ref, fv_ref = refs[:5]
    piece_refs = refs[5 : 5 + len(starts)]
    rest = refs[5 + len(starts) :]
    if earlier:
        old_ref, old_top_ref, old_sum_ref = rest[:3]
    k_ref, v_ref = rest[-2:]
    if fetch:
        raw_ref, raw_sem = rest[-4:-2]
        rest = rest[:-2]
    if last:
        out_ref, held_ref, sem = rest[-5:-2]
    else:
        o_ref, top_ref, sum_ref = rest[-5:-2]
    scale = HD**-0.5 * LOG2E
    heads = HEADS
    parts = []
    for piece_ref, start in zip(piece_refs, starts):
        if len(piece_ref.shape) == 4:
            parts += [(piece_ref.at[i], start) for i in range(piece_ref.shape[0])]
        else:
            parts.append((piece_ref, start))
    tokens = parts[0][0].shape[-2]
    cached = len(parts) * tokens
    nt = (((1,), (1,)), ((), ()))
    shape = (heads * C, C)
    token = lax.rem(lax.broadcasted_iota(jnp.int32, shape, 0), C)
    causal = lax.broadcasted_iota(jnp.int32, shape, 1) <= token
    filled = token < filled_ref[0]

    def span(start, size):
        return pl.ds(start * HD, size * HD)

    def store(h, g):
        return pltpu.make_async_copy(
            held_ref.at[:, span(h * GROUP + g, heads)],
            out_ref.at[:, span((first + h) * GROUP + g, heads)],
            sem.at[h * (GROUP // heads) + g // heads],
        )

    def load(p):
        piece_ref, start = parts[p]
        cols = pl.ds((first - start) * HD, count * HD)
        return pltpu.make_async_copy(
            piece_ref.at[:, :, cols], raw_ref.at[p], raw_sem.at[p]
        )

    if fetch:
        for p in range(len(parts)):
            load(p).start()

    def part(p, kind, h):
        if fetch:
            return raw_ref[p, kind, :, span(h, 1)]
        piece_ref, start = parts[p]
        return piece_ref[kind, :, span(first + h - start, 1)]

    def one_head(h):
        head = first + h
        base = head * GROUP
        fk = fk_ref[:, span(head, 1)]
        for p in range(len(parts)):
            at = slice(p * tokens, (p + 1) * tokens)
            if fetch and h == 0:
                load(p).wait()
            live = live_ref[rows * cached + p * tokens : rows * cached + (p + 1) * tokens]
            k_ref[at] = jnp.where(live > 0, part(p, 0, h), fk[:1])
            v_ref[at, :HD] = jnp.where(live > 0, part(p, 1, h), jnp.zeros_like(live))
            v_ref[at, HD:] = live
        if fresh:
            k_ref[cached:] = fk
            v_ref[cached:, :HD] = fv_ref[:, span(head, 1)]
            v_ref[cached:, HD:] = jnp.ones_like(fk)

        def scores(g):
            q = [q_ref[:, span(base + i, 1)] for i in range(g, g + heads)]
            q = jnp.concatenate(q, axis=0)
            return lax.dot_general(q, k_ref[...], nt, preferred_element_type=jnp.float32)

        def old(ref, many):
            return jnp.concatenate([ref[:, span(h * GROUP + i, 1)] for i in many], axis=0)

        ahead = scores(0)
        for g in range(0, GROUP, heads):
            many = range(g, g + heads)
            s = ahead
            if g + heads < GROUP:
                ahead = scores(g + heads)
            blocks = [s[:, i : i + HD] for i in range(0, s.shape[1], HD)]
            if fresh:
                blocks[-1] = jnp.where(causal, blocks[-1], NEG)
            top = functools.reduce(jnp.maximum, blocks)
            top = jnp.broadcast_to(jnp.max(top, axis=1, keepdims=True), top.shape)
            if earlier:
                old_top = old(old_top_ref, many)
                top = jnp.maximum(top, old_top)
            p = [jnp.exp2((b - top) * scale).astype(jnp.bfloat16) for b in blocks]
            p = jnp.concatenate(p, axis=1)
            o = jnp.dot(p, v_ref[...], preferred_element_type=jnp.float32)
            o, total = o[:, :HD], o[:, HD:]
            if earlier:
                share = jnp.exp2((old_top - top) * scale)
                o = o + share * old(old_ref, many)
                total = total + share * old(old_sum_ref, many)
            if last:
                o = jnp.where(filled, o / total, 0.0).astype(held_ref.dtype)
            for k, i in enumerate(many):
                at = slice(k * C, (k + 1) * C)
                if last:
                    held_ref[:, span(h * GROUP + i, 1)] = o[at]
                else:
                    col = span(h * GROUP + i, 1)
                    o_ref[:, col] = o[at]
                    top_ref[:, col] = top[at]
                    sum_ref[:, col] = total[at]
            if last:
                store(h, g).start()

    for h in range(count):
        one_head(h)
    if last:
        for h in range(count):
            for g in range(0, GROUP, heads):
                store(h, g).wait()


def attend(first, count, filled, live, queries, fresh_k, fresh_v, pieces, rows, out=None, earlier=None, fresh=True, last=True, fetch=True):
    width = GROUP * HD
    tokens = sum(
        p.shape[-2] * (p.shape[0] if p.ndim == 4 else 1) for p, start in pieces
    )
    operands = [filled, live, queries, fresh_k, fresh_v]
    operands += [
        pltpu.with_memory_space_constraint(p, pltpu.HBM) if fetch else p
        for p, start in pieces
    ]
    if earlier is not None:
        operands += earlier
    inside = pl.BlockSpec(memory_space=pltpu.VMEM)
    outside = pl.BlockSpec(memory_space=pltpu.HBM)
    in_specs = [pl.BlockSpec(memory_space=pltpu.SMEM)] + [inside] * (len(operands) - 1)
    if fetch:
        in_specs[5 : 5 + len(pieces)] = [outside] * len(pieces)
    aliases = {}
    if out is not None:
        operands.append(out)
        in_specs.append(pl.BlockSpec(memory_space=pl.ANY))
        aliases = {len(operands) - 1: 0}
    keys = tokens + (C if fresh else 0)
    each = pieces[0][0].shape[-2]
    scratch_shapes = [
        pltpu.VMEM((keys, HD), jnp.bfloat16),
        pltpu.VMEM((keys, 2 * HD), jnp.bfloat16),
    ]
    if fetch:
        scratch_shapes = [
            pltpu.VMEM((tokens // each, 2, each, count * HD), jnp.bfloat16),
            pltpu.SemaphoreType.DMA((tokens // each,)),
        ] + scratch_shapes
    if last:
        out_shape = pltpu.HBM((C, H * HD), jnp.bfloat16)
        out_specs = pl.BlockSpec(memory_space=pltpu.HBM)
        scratch_shapes = [
            pltpu.VMEM((C, count * width), jnp.bfloat16),
            pltpu.SemaphoreType.DMA((count * GROUP // HEADS,)),
        ] + scratch_shapes
    else:
        out_shape = [
            jax.ShapeDtypeStruct((C, count * width), jnp.float32)
        ] * 3
        out_specs = [inside] * 3
    return pl.pallas_call(
        functools.partial(
            attend_kernel,
            first=first,
            count=count,
            starts=tuple(start for p, start in pieces),
            rows=rows,
            fresh=fresh,
            earlier=earlier is not None,
            last=last,
            fetch=fetch,
        ),
        out_shape=out_shape,
        in_specs=in_specs,
        out_specs=out_specs,
        scratch_shapes=scratch_shapes,
        input_output_aliases=aliases,
        compiler_params=pltpu.CompilerParams(vmem_limit_bytes=16 * 2**20),
        cost_estimate=pl.CostEstimate(
            flops=4 * count * C * width * keys,
            bytes_accessed=4 * count * C * width * 2,
            transcendentals=count * C * GROUP * keys,
        ),
        name=f"attend_{first}_{rows}",
    )(*operands)


def local(queries, fresh_kv, kv_pool, page_holder, page_slot, cached_len, fresh_len):
    devices = lax.axis_size("dp")
    chips = devices // 2
    me = lax.axis_index("dp")
    flip = chips <= MOST_PERMUTES
    same_core = [[2 * i + core for i in range(chips)] for core in range(2)]
    mate_pool = lax.ppermute(kv_pool, "dp", [(i, i ^ 1) for i in range(devices)])
    asked = ask(me.reshape(1), page_holder, page_slot, chips)
    exchange = functools.partial(
        lax.all_to_all,
        axis_name="dp",
        split_axis=0,
        concat_axis=0,
        axis_index_groups=same_core,
        tiled=True,
    )
    wanted = exchange(asked)
    own_pool = pltpu.with_memory_space_constraint(kv_pool, pltpu.HBM)
    mate_pool = pltpu.with_memory_space_constraint(mate_pool, pltpu.VMEM)
    mine = (me >> 1).reshape(1)
    gather = functools.partial(gather_pages, mine, wanted, own_pool, mate_pool)
    order = (me if flip else me & 1).reshape(1)
    live = live_tokens(order, cached_len, page_holder, MP // devices)
    fresh_k, fresh_v = fresh_kv[0, :, 0], fresh_kv[0, :, 1]

    def attend_some(first, count, pieces, *args, **kwargs):
        pieces = [
            (p.reshape(p.shape[:-3] + (-1, p.shape[-1])), start) for p, start in pieces
        ]
        return attend(
            first, count, fresh_len, live, queries[0], fresh_k, fresh_v, pieces, *args, **kwargs
        )

    out = None
    if not flip:
        sent = gather([(None, first, count) for first, count in CHUNKS])
        for (first, count), piece in zip(CHUNKS, sent):
            out = attend_some(first, count, [(exchange(piece), first)], 0, out)
        return out[None]

    def swap(piece, x):
        return lax.ppermute(piece, "dp", [(i, i ^ 2 * x) for i in range(devices)])

    near, far = range(chips // 2), range(chips // 2, chips)
    sent = gather(
        [(x, 0, KVH) for x in near]
        + [(x, first, count) for first, count in CHUNKS for x in far]
    )
    close = [(sent[x] if x == 0 else swap(sent[x], x), 0) for x in near]
    arrived = []
    for c, (first, count) in enumerate(CHUNKS):
        batch = sent[len(near) + c * len(far) : len(near) + (c + 1) * len(far)]
        if c > 0:
            batch = hold_back(batch, arrived[:1])
        arrived = [swap(piece, x) for piece, x in zip(batch, far)]
        pieces = [(piece, first) for piece in arrived]
        if c < len(CHUNKS) - 1:
            out = attend_some(first, count, close + pieces, 0, out)
        else:
            earlier = attend_some(first, count, close, 0, last=False)
            out = attend_some(
                first, count, pieces, 1, out, earlier=earlier, fresh=False, fetch=False
            )
    return out[None]


def solution(mesh):
    return jax.shard_map(
        local,
        mesh=mesh,
        in_specs=(
            P(("groups", "dp"), None, None),
            P(("groups", "dp"), None, None, None),
            P(("groups", "dp"), None, None, None),
            P(("groups", "dp"), None),
            P(("groups", "dp"), None),
            P(("groups", "dp")),
            P(("groups", "dp")),
        ),
        out_specs=P(("groups", "dp"), None, None),
        check_vma=False,
    )
```
